128 devices in a mesh: ctx: 64 (over z_hi, x, y, core), fsdp: 2 (over z_lo).
Axes of the slice: x: 4, y: 4, z: 4 (z_hi: 2, z_lo: 2; z = z_hi * 2 + z_lo), core: 2. Of those that a mesh axis runs over, the one named last changes fastest.
Arguments:
- layer_in: bfloat16 [16384, 960], P(('ctx', 'fsdp')), may hold values from -6 to 6
- attn_gain: bfloat16 [960], P('ctx'), may hold values from 0.5 to 1.5
- query_weight: bfloat16 [960, 960], P('ctx', 'fsdp'), may hold values from -0.1875 to 0.1875
- key_weight: bfloat16 [960, 320], P('ctx', 'fsdp'), may hold values from -0.1875 to 0.1875
- value_weight: bfloat16 [960, 320], P('ctx', 'fsdp'), may hold values from -0.1875 to 0.1875
- output_weight: bfloat16 [960, 960], P('ctx', 'fsdp'), may hold values from -1.5 to 1.5
- ffn_gain: bfloat16 [960], P('ctx'), may hold values from 0.5 to 1.5
- gate_weight: bfloat16 [960, 2560], P('ctx', 'fsdp'), may hold values from -0.1875 to 0.1875
- up_weight: bfloat16 [960, 2560], P('ctx', 'fsdp'), may hold values from -0.1875 to 0.1875
- down_weight: bfloat16 [2560, 960], P('ctx', 'fsdp'), may hold values from -0.125 to 0.125
- out_cotangent: bfloat16 [16384, 960], P(('ctx', 'fsdp')), may hold values from -6 to 6
Outputs:
- layer_out: bfloat16 [16384, 960], P(('ctx', 'fsdp'))
- input_grad: float32 [16384, 960], P(('ctx', 'fsdp'))
- attn_gain_grad: float32 [960], P('ctx')
- query_grad: float32 [960, 960], P('ctx', 'fsdp')
- key_grad: float32 [960, 320], P('ctx', 'fsdp')
- value_grad: float32 [960, 320], P('ctx', 'fsdp')
- output_grad: float32 [960, 960], P('ctx', 'fsdp')
- ffn_gain_grad: float32 [960], P('ctx')
- gate_grad: float32 [960, 2560], P('ctx', 'fsdp')
- up_grad: float32 [960, 2560], P('ctx', 'fsdp')
- down_grad: float32 [2560, 960], P('ctx', 'fsdp')
The draws below stay inside these ranges and needn't reach their ends.
All inputs are finite; a program needn't handle non-finite values.
Results may differ from the reference program's by a relative error of at most 0.04.
Values may be sent and summed in bfloat16 or wider, within the bound.
A program may use at most 448 MiB of HBM per device.

```python
import jax
import jax.numpy as jnp
from jax import lax

D = 960
QH = 15
KEY_HEADS = 5
HEAD_SIZE = 64
FF = 2560
QW = 960
KW = 320
TOKENS = 16384


def steps_of(own_key, extent, cuts, least, largest):
    def one(dim, shards_of):
        steps = jax.random.uniform(jax.random.fold_in(jax.random.fold_in(own_key, 6), dim), (shards_of,), jnp.float32, least / len(cuts), largest / len(cuts))
        return jnp.repeat(jnp.exp(steps), extent[dim] // shards_of).reshape((-1,) + (1,) * (len(extent) - dim - 1))

    level = one(*cuts[0])
    for cut in cuts[1:]:
        level = level * one(*cut)
    return level


def bell_draw(rng, dims, scale, reach, shards=(), held_as=jnp.bfloat16):
    values = scale * jax.random.normal(rng, dims, jnp.float32)
    if shards:
        values = values * steps_of(rng, dims, shards, -0.22, 0.18)
    return jnp.clip(values, -reach, reach).astype(held_as)


def setup_inputs(seed: int = 0) -> dict:
    arg_keys = jax.random.split(jax.random.key(seed), 12)
    layer_in = bell_draw(arg_keys[0], (TOKENS, D), 1.0, 6.0, ((0, 128),))
    attn_gain = jnp.clip(1.0 + 0.1 * jax.random.normal(arg_keys[1], (D,), jnp.float32), 0.5, 1.5).astype(jnp.bfloat16)
    query_weight = bell_draw(arg_keys[2], (D, QW), D ** -0.5, 0.1875, ((0, 64), (1, 2)))
    key_weight = bell_draw(arg_keys[3], (D, KW), D ** -0.5, 0.1875, ((0, 64), (1, 2)))
    value_weight = bell_draw(arg_keys[4], (D, KW), D ** -0.5, 0.1875, ((0, 64), (1, 2)))
    output_weight = bell_draw(arg_keys[5], (QW, D), (max(QW // 64, 1)) ** -0.5, 1.5, ((0, 64), (1, 2)))
    ffn_gain = jnp.clip(1.0 + 0.1 * jax.random.normal(arg_keys[6], (D,), jnp.float32), 0.5, 1.5).astype(jnp.bfloat16)
    gate_weight = bell_draw(arg_keys[7], (D, FF), D ** -0.5, 0.1875, ((0, 64), (1, 2)))
    up_weight = bell_draw(arg_keys[8], (D, FF), D ** -0.5, 0.1875, ((0, 64), (1, 2)))
    down_weight = bell_draw(arg_keys[9], (FF, D), FF ** -0.5, 0.125, ((0, 64), (1, 2)))
    out_cotangent = bell_draw(arg_keys[10], (TOKENS, D), 1.0, 6.0, ((0, 128),))
    return dict(layer_in=layer_in, attn_gain=attn_gain, query_weight=query_weight, key_weight=key_weight, value_weight=value_weight, output_weight=output_weight, ffn_gain=ffn_gain, gate_weight=gate_weight, up_weight=up_weight, down_weight=down_weight, out_cotangent=out_cotangent)


EPS = 1e-05
ROPE_BASE = 10000.0
NEGATIVE = -1e+30
HIGH_PRECISION = lax.Precision.HIGHEST

@jax.custom_vjp
def low(v):
    return lax.optimization_barrier(v.astype(jnp.bfloat16)).astype(jnp.float32)

@jax.custom_vjp
def low_back(v):
    return v

def low_keep(v):
    return (low(v), None)

def low_pass(kept, grad):
    return (grad,)

def back_keep(v):
    return (v, None)

def back_low(kept, grad):
    return (low(grad),)
low.defvjp(low_keep, low_pass)
low_back.defvjp(back_keep, back_low)

def rotary(values, positions):
    count = values.shape[0]
    half = HEAD_SIZE // 2
    heads = values.reshape(count, -1, HEAD_SIZE)
    freq = ROPE_BASE ** (-(jnp.arange(half, dtype=jnp.float32) * 2.0 / HEAD_SIZE))
    angle = positions.astype(jnp.float32)[:, None] * freq[None, :]
    cosine = jnp.cos(angle)[:, None, :]
    sine = jnp.sin(angle)[:, None, :]
    first = heads[..., :half]
    second = heads[..., half:]
    turned = jnp.concatenate([first * cosine - second * sine, second * cosine + first * sine], -1)
    return turned.reshape(count, -1)

def normalize(hidden, gain):
    return hidden * lax.rsqrt(lax.optimization_barrier(jnp.mean(hidden * hidden, -1, keepdims=True)) + EPS) * gain

def attention(query_rot, key_rot, value_low):
    block = min(512, TOKENS)
    count = TOKENS // block
    groups = QH // KEY_HEADS
    score_scale = HEAD_SIZE ** (-0.5)
    key_head_rows = key_rot.reshape(TOKENS, KEY_HEADS, HEAD_SIZE)
    value_head_rows = value_low.reshape(TOKENS, KEY_HEADS, HEAD_SIZE)
    key_pos = jnp.arange(TOKENS, dtype=jnp.int32)

    def one_block(inputs):
        query_block, start = inputs
        query_head_rows = query_block.reshape(block, KEY_HEADS, groups, HEAD_SIZE)
        attention_logits = jnp.einsum('amxb,jmb->mxaj', query_head_rows, key_head_rows, precision=HIGH_PRECISION) * score_scale
        attention_logits = low_back(attention_logits)
        query_pos = start + jnp.arange(block, dtype=jnp.int32)
        mask = query_pos[:, None] >= key_pos[None, :]
        attention_logits = jnp.where(mask, attention_logits, NEGATIVE)
        probabilities = low(jax.nn.softmax(attention_logits, -1))
        final_output = jnp.einsum('bche,ebq->hbcq', probabilities, value_head_rows, precision=HIGH_PRECISION)
        return final_output.reshape(block, QW)
    starts = (jnp.arange(count, dtype=jnp.int32) * block).astype(jnp.int32)
    blocks = query_rot.reshape(count, block, QW)
    return lax.map(jax.checkpoint(one_block), (blocks, starts)).reshape(TOKENS, QW)

def layer(hidden, attn_gain, query_weight, key_weight, value_weight, output_weight, ffn_gain, gate_weight, up_weight, down_weight):
    positions = jnp.arange(TOKENS, dtype=jnp.int32)
    normed = low(normalize(hidden, attn_gain))
    query = low_back(jnp.dot(normed, query_weight, precision=HIGH_PRECISION))
    key = low_back(jnp.dot(normed, key_weight, precision=HIGH_PRECISION))
    value = low_back(jnp.dot(normed, value_weight, precision=HIGH_PRECISION))
    query_rot = low(rotary(query, positions))
    key_rot = low(rotary(key, positions))
    value_low = low(value)
    attended = low(low_back(attention(query_rot, key_rot, value_low)))
    middle = hidden + low_back(jnp.dot(attended, output_weight, precision=HIGH_PRECISION))
    normed_two = low(normalize(middle, ffn_gain))
    gate = low_back(jnp.dot(normed_two, gate_weight, precision=HIGH_PRECISION))
    upward = low_back(jnp.dot(normed_two, up_weight, precision=HIGH_PRECISION))
    inner = low(jax.nn.silu(gate) * upward)
    return middle + low_back(jnp.dot(inner, down_weight, precision=HIGH_PRECISION))

def reference(layer_in, attn_gain, query_weight, key_weight, value_weight, output_weight, ffn_gain, gate_weight, up_weight, down_weight, out_cotangent):
    primals = tuple((a.astype(jnp.float32) for a in (layer_in, attn_gain, query_weight, key_weight, value_weight, output_weight, ffn_gain, gate_weight, up_weight, down_weight)))
    final_output, pull = jax.vjp(layer, *primals)
    grads = pull(out_cotangent.astype(jnp.float32))
    return (final_output.astype(jnp.bfloat16), grads[0], grads[1], grads[2], grads[3], grads[4], grads[5], grads[6], grads[7], grads[8], grads[9])
```

```python
import functools

import jax
import jax.numpy as jnp
from jax import lax
from jax.experimental import pallas as pl
from jax.experimental.pallas import tpu as pltpu
from jax.sharding import PartitionSpec as P

MESH = pl.DeviceIdType.MESH
ORDERS = (("x", "y", "z"), ("y", "z", "x"), ("z", "x", "y"))
ALL = slice(None)


def whereabouts():
    ctx = lax.axis_index("ctx")
    low = lax.axis_index("fsdp")
    return {
        "x": lax.rem(lax.div(ctx, 8), 4),
        "y": lax.rem(lax.div(ctx, 2), 4),
        "z": lax.div(ctx, 32) * 2 + low,
        "c": lax.rem(ctx, 2),
    }


def device_at(at):
    ctx = ((lax.div(at["z"], 2) * 4 + at["x"]) * 4 + at["y"]) * 2 + at["c"]
    return (ctx, lax.rem(at["z"], 2))


def moved(at, axis, by):
    size = 2 if axis == "c" else 4
    return {**at, axis: lax.rem(at[axis] + by + size, size)}


def greet(me):
    barrier = pltpu.get_barrier_semaphore()
    others = [moved(me, a, s) for a in "xyz" for s in (1, -1)] + [moved(me, "c", 1)]
    for other in others:
        pl.semaphore_signal(barrier, inc=1, device_id=device_at(other), device_id_type=MESH)
    pl.semaphore_wait(barrier, len(others))


def place(dims, at):
    index = []
    for d in dims:
        if d in ("zh", "zl"):
            z = at["z"]
            index.append(ALL if z is ALL else (lax.div(z, 2) if d == "zh" else lax.rem(z, 2)))
        elif d == "l":
            index.append(at.get("l", ALL))
        else:
            index.append(at[d])
    return index


def view(ref, dims, at, cols, half=None):
    start, width = cols
    if half is not None:
        if "l" in dims:
            at = {**at, "l": half}
        else:
            start, width = start + half * (width // 2), width // 2
    return ref.at[tuple(place(dims, at)) + (ALL, pl.ds(start, width))]


def gather_kernel(dims, parts, piece_ref, out_ref, send, recv, sib_send, sib_recv, own_sem):
    me = whereabouts()
    greet(me)
    sibling = device_at(moved(me, "c", 1))
    lead = (ALL,) if "l" in dims else ()

    def copy(src, dst, ssem, rsem, to):
        c = pltpu.make_async_remote_copy(
            src_ref=src, dst_ref=dst, send_sem=ssem, recv_sem=rsem, device_id=to, device_id_type=MESH
        )
        c.start()
        return c

    pending = []
    mine = out_ref.at[tuple(place(dims, me)) + (ALL, ALL)]
    own = pltpu.make_async_copy(piece_ref, mine, own_sem)
    own.start()
    own.wait()
    for phase in range(3):
        stage = {}
        for i, cols in enumerate(parts):
            order = ORDERS[i]
            axis = order[phase]
            base = dict(me)
            for done in order[:phase]:
                base[done] = ALL
            right, left = moved(me, axis, 1), moved(me, axis, -1)

            def blk(by, half=None, base=base, axis=axis, cols=cols):
                at = {**base, axis: lax.rem(me[axis] + by + 4, 4)}
                return view(out_ref, dims, at, cols, half)

            s, r = send.at[i, phase], recv.at[i, phase]
            to_right = copy(blk(0), blk(0), s.at[0], r.at[0], device_at(right))
            to_left = copy(blk(0), blk(0), s.at[1], r.at[1], device_at(left))
            sibs = []
            if phase == 2:
                sibs.append(copy(blk(0), blk(0), sib_send.at[i, 0], sib_recv.at[i, 0], sibling))
            stage[i] = (blk, s, r, to_right, to_left, sibs, right, left)
        for i in range(len(parts)):
            blk, s, r, to_right, to_left, sibs, right, left = stage[i]
            to_right.wait_recv()
            on_right = copy(blk(-1, 0), blk(-1, 0), s.at[2], r.at[2], device_at(right))
            if phase == 2:
                sibs.append(copy(blk(-1), blk(-1), sib_send.at[i, 1], sib_recv.at[i, 1], sibling))
            to_left.wait_recv()
            on_left = copy(blk(1, 1), blk(1, 1), s.at[3], r.at[3], device_at(left))
            if phase == 2:
                sibs.append(copy(blk(1), blk(1), sib_send.at[i, 2], sib_recv.at[i, 2], sibling))
            pending += [to_right, to_left, on_right, on_left]
            stage[i] = (blk, sibs, on_right, on_left)
        for i in range(len(parts)):
            blk, sibs, on_right, on_left = stage[i]
            on_right.wait_recv()
            on_left.wait_recv()
            if phase == 2:
                sibs.append(copy(blk(2), blk(2), sib_send.at[i, 3], sib_recv.at[i, 3], sibling))
                pending += sibs
        if phase == 2:
            for i in range(len(parts)):
                for c in stage[i][1]:
                    c.wait_recv()
    for c in pending:
        c.wait_send()


SIZE = {"zl": 2, "zh": 2, "x": 4, "y": 4, "c": 2, "l": 2}


def gather(piece, dims, parts, name, collective_id):
    shape = tuple(SIZE[d] for d in dims) + piece.shape[-2:]
    n = len(parts)
    return pl.pallas_call(
        functools.partial(gather_kernel, dims, parts),
        out_shape=jax.ShapeDtypeStruct(shape, piece.dtype),
        in_specs=[pl.BlockSpec(memory_space=pl.ANY)],
        out_specs=pl.BlockSpec(memory_space=pl.ANY),
        scratch_shapes=[
            pltpu.SemaphoreType.DMA((n, 3, 4)),
            pltpu.SemaphoreType.DMA((n, 3, 4)),
            pltpu.SemaphoreType.DMA((n, 4)),
            pltpu.SemaphoreType.DMA((n, 4)),
            pltpu.SemaphoreType.DMA,
        ],
        compiler_params=pltpu.CompilerParams(collective_id=collective_id, has_side_effects=True),
        name=name,
    )(piece)


def scatter_kernel(dims, parts, n_in, *refs):
    ins, out_ref, refs = refs[:n_in], refs[n_in], refs[n_in + 1 :]
    n = len(parts)
    work, sib = refs[:n], refs[n : 2 * n]
    bufs = refs[2 * n : 2 * n + 12 * n]
    load_sem, sib_send, sib_recv, send, recv = refs[14 * n :]
    wdims = tuple(d for d in dims if d != "c")
    me = whereabouts()
    other = moved(me, "c", 1)
    sibling = device_at(other)
    widths = [w.shape[-1] for w in work]
    starts = [sum(widths[:i]) for i in range(n)]

    def remote(src, dst, ssem, rsem, to):
        c = pltpu.make_async_remote_copy(
            src_ref=src, dst_ref=dst, send_sem=ssem, recv_sem=rsem, device_id=to, device_id_type=MESH
        )
        c.start()
        return c

    loads, pairs = {}, {}
    TURN = (2, 1, -1, 0)

    def own_loads(step):
        for i, sources in enumerate(parts):
            axis = ORDERS[i][0]
            at = {"x": ALL, "y": ALL, "z": ALL, "c": me["c"], axis: lax.rem(me[axis] + TURN[step] + 4, 4)}
            loads[i, step] = []
            for j, (k, (c0, width), d0) in enumerate(sources):
                c = pltpu.make_async_copy(
                    view(ins[k], dims, at, (c0, width)),
                    view(work[i], wdims, at, (d0, width)),
                    load_sem.at[i, step, j],
                )
                c.start()
                loads[i, step].append(c)

    def sib_sends(step):
        for i, sources in enumerate(parts):
            axis = ORDERS[i][0]
            at = {"x": ALL, "y": ALL, "z": ALL, "c": other["c"], axis: lax.rem(me[axis] + TURN[step] + 4, 4)}
            pairs[i, step] = []
            for j, (k, (c0, width), d0) in enumerate(sources):
                pairs[i, step].append(
                    remote(
                        view(ins[k], dims, at, (c0, width)),
                        view(sib[i], wdims, at, (d0, width)),
                        sib_send.at[i, step, j],
                        sib_recv.at[i, step, j],
                        sibling,
                    )
                )

    own_loads(0)
    greet(me)
    for step in range(4):
        sib_sends(step)
        if step:
            own_loads(step)
    pending = []

    def each_block(at, body):
        free = [d for d in wdims if (at["z"] if d in ("zh", "zl") else at.get(d, ALL)) is ALL]
        total = 1
        for d in free:
            total *= SIZE[d]

        def one(t, _):
            vals, rest = {}, t
            for d in reversed(free):
                vals[d] = lax.rem(rest, SIZE[d])
                rest = lax.div(rest, SIZE[d])
            full = []
            for d, fixed in zip(wdims, place(wdims, at)):
                full.append(vals[d] if d in vals else fixed)
            body(tuple(full), tuple(vals[d] for d in free))
            return 0

        if total == 1:
            one(jnp.int32(0), 0)
        else:
            lax.fori_loop(0, total, one, 0)

    f32 = jnp.float32

    def add(i, at, others, half=None, out=None):
        w = widths[i]
        lo, size = 0, w
        if half is not None:
            if "l" in wdims:
                at = {**at, "l": half}
            else:
                lo, size = half * (w // 2), w // 2

        def body(full, short):
            cut = (ALL, pl.ds(lo, size))
            total = work[i][full + cut].astype(f32)
            for ref, same in others:
                if same:
                    total = total + ref[full + cut].astype(f32)
                else:
                    total = total + ref[short + (ALL, ALL)].astype(f32)
            if out is None:
                work[i][full + cut] = total.astype(work[i].dtype)
            else:
                lead = (full[0],) if "l" in wdims else ()
                out[lead + (ALL, pl.ds(starts[i], w))] = total

        each_block(at, body)

    for phase in range(3):
        stage = {}

        def ctx_of(i):
            order = ORDERS[i]
            axis = order[phase]
            base = {"x": ALL, "y": ALL, "z": ALL}
            for done in order[:phase]:
                base[done] = me[done]
            return axis, base

        def at_of(i, by):
            axis, base = ctx_of(i)
            return {**base, axis: lax.rem(me[axis] + by + 4, 4)}

        def ready(i, step):
            if phase == 0:
                for c in loads[i, step]:
                    c.wait()
                for c in pairs[i, step]:
                    c.wait_recv()
                add(i, at_of(i, TURN[step]), [(sib[i], True)])

        for i in range(n):
            axis, _ = ctx_of(i)
            b = bufs[12 * i + 4 * phase : 12 * i + 4 * phase + 4]
            s, r = send.at[i, phase], recv.at[i, phase]
            ready(i, 0)
            right, left = device_at(moved(me, axis, 1)), device_at(moved(me, axis, -1))
            far = at_of(i, 2)
            one = remote(view(work[i], wdims, far, (0, widths[i]), 0), b[0], s.at[0], r.at[0], right)
            two = remote(view(work[i], wdims, far, (0, widths[i]), 1), b[1], s.at[1], r.at[1], left)
            stage[i] = [b, s, r, right, left, one, two]
        for i in range(n):
            b, s, r, right, left, one, two = stage[i]
            ready(i, 1)
            one.wait_recv()
            add(i, at_of(i, 1), [(b[0], False)], 0)
            three = remote(view(work[i], wdims, at_of(i, 1), (0, widths[i])), b[2], s.at[2], r.at[2], right)
            ready(i, 2)
            two.wait_recv()
            add(i, at_of(i, -1), [(b[1], False)], 1)
            four = remote(view(work[i], wdims, at_of(i, -1), (0, widths[i])), b[3], s.at[3], r.at[3], left)
            stage[i] = [b, three, four]
            pending += [one, two, three, four]
        for i in range(n):
            b, three, four = stage[i]
            ready(i, 3)
            three.wait_recv()
            four.wait_recv()
            add(i, at_of(i, 0), [(b[2], False), (b[3], False)], None, out_ref if phase == 2 else None)
    for c in pending:
        c.wait_send()
    for k in pairs:
        for c in pairs[k]:
            c.wait_send()


def scatter(ins, dims, parts, rows, name, collective_id, vmem):
    n = len(parts)
    wdims = tuple(d for d in dims if d != "c")
    widths = [sum(width for _, (_, width), _ in sources) for sources in parts]
    wshape = tuple(SIZE[d] for d in wdims)
    dt = ins[0].dtype
    scratch = [pltpu.VMEM(wshape + (rows, w), dt) for w in widths] * 2
    for i in range(n):
        for phase in range(3):
            gone = set(ORDERS[i][: phase + 1])
            left = [d for d in wdims if ("z" if d in ("zh", "zl") else d) not in gone]
            shape = tuple(SIZE[d] for d in left)
            small = tuple(SIZE[d] for d in left if d != "l")
            halfw = widths[i] if "l" in dims else widths[i] // 2
            scratch += [pltpu.VMEM(small + (rows, halfw), dt)] * 2
            scratch += [pltpu.VMEM(shape + (rows, widths[i]), dt)] * 2
    most = max(len(s) for s in parts)
    scratch += [
        pltpu.SemaphoreType.DMA((n, 4, most)),
        pltpu.SemaphoreType.DMA((n, 4, most)),
        pltpu.SemaphoreType.DMA((n, 4, most)),
        pltpu.SemaphoreType.DMA((n, 3, 4)),
        pltpu.SemaphoreType.DMA((n, 3, 4)),
    ]
    lead = (2,) if "l" in dims else ()
    return pl.pallas_call(
        functools.partial(scatter_kernel, dims, parts, len(ins)),
        out_shape=jax.ShapeDtypeStruct(lead + (rows, sum(widths)), jnp.float32),
        in_specs=[pl.BlockSpec(memory_space=pl.ANY)] * len(ins),
        out_specs=pl.BlockSpec(memory_space=pltpu.VMEM),
        scratch_shapes=scratch,
        compiler_params=pltpu.CompilerParams(
            collective_id=collective_id, has_side_effects=True, vmem_limit_bytes=vmem
        ),
        name=name,
    )(*ins)


W_DIMS = ("zl", "zh", "x", "y", "c")
W_PARTS = ((0, 1792), (1792, 1792), (3584, 1792))
T_DIMS = ("l", "zh", "x", "y", "c", "zl")
T_PARTS = ((0, 256), (256, 256), (512, 128))


QH = 15
KEY_HEADS = 5
GROUPS = 3
HEAD_SIZE = 64
EPS = 1e-05
ROPE_BASE = 10000.0
NEGATIVE = -1e30
LOG2E = 1.4426950408889634
BLOCKS = 128
HALF = 64
SIDE = BLOCKS * HALF
LANES = GROUPS * HALF
CHUNK = 512
VMEM_LIMIT = 56 << 20


def chunk_ranges(side, own):
    count = SIDE // CHUNK
    if side == 0:
        diag = lax.div(HALF * own, CHUNK)
        first = HALF * (BLOCKS - own)
        edge, whole = lax.div(first, CHUNK), lax.div(first + CHUNK - 1, CHUNK)
        return ((diag, diag + 1), (0, diag)), ((edge, whole), (whole, count))
    rows = HALF * (own + 1)
    edge, whole = lax.div(rows, CHUNK), lax.div(rows + CHUNK - 1, CHUNK)
    diag = lax.div(HALF * (BLOCKS - 1 - own), CHUNK)
    return ((edge, whole), (0, edge)), ((diag, diag + 1), (diag + 1, count))


def seen(source, chunk, side, own):
    row = chunk * CHUNK + lax.broadcasted_iota(jnp.int32, (CHUNK, LANES), 0)
    block, place = row // HALF, row % HALF
    if source == 0:
        key = block * (2 * HALF) + place
    else:
        key = (BLOCKS - 1 - block) * (2 * HALF) + HALF + place
    col = lax.broadcasted_iota(jnp.int32, (CHUNK, LANES), 1)
    return key <= own * (2 * HALF) + side * HALF + col % HALF


def dot_nt(a, b):
    return lax.dot_general(a, b, (((1,), (1,)), ((), ())), preferred_element_type=jnp.float32)


def dot_tn(a, b):
    return lax.dot_general(a, b, (((0,), (0,)), ((), ())), preferred_element_type=jnp.float32)


def dot_nn(a, b):
    return lax.dot_general(a, b, (((1,), (0,)), ((), ())), preferred_element_type=jnp.float32)


def my_block():
    return lax.axis_index("ctx") * 2 + lax.axis_index("fsdp")


def attend_kernel(kv_ref, q_ref, o_ref, lse_ref, acc_ref):
    me = my_block()
    for side in range(2):
        own = me if side == 0 else BLOCKS - 1 - me
        q = q_ref[0, side]
        acc_ref[...] = jnp.zeros_like(acc_ref)
        carry = (jnp.full((1, LANES), NEGATIVE, jnp.float32), jnp.zeros((1, LANES), jnp.float32))

        def step(source, masked, chunk, carry):
            peak, total = carry
            kv = kv_ref[source, pl.ds(pl.multiple_of(chunk * CHUNK, CHUNK), CHUNK), :]
            s = dot_nt(kv, q) * LOG2E
            if masked:
                s = jnp.where(seen(source, chunk, side, own), s, NEGATIVE)
            new = jnp.maximum(peak, jnp.max(s, 0, keepdims=True))
            p = jnp.exp2(s - new)
            scale = jnp.exp2(peak - new)
            total = total * scale + jnp.sum(p, 0, keepdims=True)
            acc_ref[...] = acc_ref[...] * scale + dot_tn(kv, p.astype(jnp.bfloat16))
            return new, total

        for source, (edge, whole) in enumerate(chunk_ranges(side, own)):
            carry = lax.fori_loop(edge[0], edge[1], functools.partial(step, source, True), carry)
            carry = lax.fori_loop(whole[0], whole[1], functools.partial(step, source, False), carry)
        peak, total = carry
        o_ref[0, side] = acc_ref[HEAD_SIZE:, :] / total
        lse_ref[0, side] = peak + jnp.log2(total)


def attend(kv, q):
    return pl.pallas_call(
        attend_kernel,
        grid=(KEY_HEADS,),
        out_shape=(
            jax.ShapeDtypeStruct((KEY_HEADS, 2, HEAD_SIZE, LANES), jnp.float32),
            jax.ShapeDtypeStruct((KEY_HEADS, 2, 1, LANES), jnp.float32),
        ),
        in_specs=[
            pl.BlockSpec((2, SIDE, 128), lambda h: (0, 0, h)),
            pl.BlockSpec((1, 2, LANES, 128), lambda h: (h, 0, 0, 0)),
        ],
        out_specs=(
            pl.BlockSpec((1, 2, HEAD_SIZE, LANES), lambda h: (h, 0, 0, 0)),
            pl.BlockSpec((1, 2, 1, LANES), lambda h: (h, 0, 0, 0)),
        ),
        scratch_shapes=[pltpu.VMEM((128, LANES), jnp.float32)],
        compiler_params=pltpu.CompilerParams(vmem_limit_bytes=VMEM_LIMIT),
        name="attend",
    )(kv, q)


def attend_back_kernel(kv_ref, q_ref, do_ref, lse_ref, delta_ref, dq_ref, dkv_ref, acc_ref):
    me = my_block()
    dkv_ref[...] = jnp.zeros_like(dkv_ref)
    for side in range(2):
        own = me if side == 0 else BLOCKS - 1 - me
        q, do = q_ref[0, side], do_ref[0, side]
        lse, delta = lse_ref[0, side], delta_ref[0, side]
        acc_ref[...] = jnp.zeros_like(acc_ref)

        def step(source, masked, chunk, carry):
            rows = pl.ds(pl.multiple_of(chunk * CHUNK, CHUNK), CHUNK)
            kv = kv_ref[source, rows, :]
            p = jnp.exp2(dot_nt(kv, q) * LOG2E - lse)
            if masked:
                p = jnp.where(seen(source, chunk, side, own), p, 0.0)
            ds = (p * (dot_nt(kv, do) - delta)).astype(jnp.bfloat16)
            more = dot_nn(ds, q) + dot_nn(p.astype(jnp.bfloat16), do)
            dkv_ref[source, rows, :] = (dkv_ref[source, rows, :].astype(jnp.float32) + more).astype(jnp.bfloat16)
            acc_ref[...] += dot_tn(kv, ds)
            return carry

        for source, (edge, whole) in enumerate(chunk_ranges(side, own)):
            lax.fori_loop(edge[0], edge[1], functools.partial(step, source, True), 0)
            lax.fori_loop(whole[0], whole[1], functools.partial(step, source, False), 0)
        dq_ref[0, side] = acc_ref[:HEAD_SIZE, :]


def attend_back(kv, q, do, lse, delta):
    per_head = pl.BlockSpec((1, 2, LANES, 128), lambda h: (h, 0, 0, 0))
    row = pl.BlockSpec((1, 2, 1, LANES), lambda h: (h, 0, 0, 0))
    keys = pl.BlockSpec((2, SIDE, 128), lambda h: (0, 0, h))
    return pl.pallas_call(
        attend_back_kernel,
        grid=(KEY_HEADS,),
        out_shape=(
            jax.ShapeDtypeStruct((KEY_HEADS, 2, HEAD_SIZE, LANES), jnp.float32),
            jax.ShapeDtypeStruct(kv.shape, jnp.bfloat16),
        ),
        in_specs=[keys, per_head, per_head, row, row],
        out_specs=(pl.BlockSpec((1, 2, HEAD_SIZE, LANES), lambda h: (h, 0, 0, 0)), keys),
        scratch_shapes=[pltpu.VMEM((128, LANES), jnp.float32)],
        compiler_params=pltpu.CompilerParams(vmem_limit_bytes=VMEM_LIMIT),
        name="attend_back",
    )(kv, q, do, lse, delta)


def rotary_tables(positions):
    half = HEAD_SIZE // 2
    freq = ROPE_BASE ** (-(jnp.arange(half, dtype=jnp.float32) * 2.0 / HEAD_SIZE))
    angle = positions.astype(jnp.float32)[:, None] * freq[None, :]
    return (jnp.cos(angle)[:, None, :], jnp.sin(angle)[:, None, :])


def rotate(values, cosine, sine):
    count = values.shape[0]
    half = HEAD_SIZE // 2
    heads = values.reshape(count, -1, HEAD_SIZE)
    first = heads[..., :half]
    second = heads[..., half:]
    return jnp.concatenate(
        [first * cosine - second * sine, second * cosine + first * sine], -1
    ).reshape(count, -1)


def mm(form, left, right):
    return jnp.einsum(form, left, right, preferred_element_type=jnp.float32)


def by_head(rows):
    r = rows.reshape(2, HALF, KEY_HEADS, GROUPS, HEAD_SIZE)
    return jnp.transpose(r, (2, 0, 3, 1, 4)).reshape(KEY_HEADS, 2, LANES, HEAD_SIZE)


def by_token(heads):
    h = heads.reshape(KEY_HEADS, 2, HEAD_SIZE, GROUPS, HALF)
    return jnp.transpose(h, (1, 4, 0, 3, 2)).reshape(2 * HALF, QH * HEAD_SIZE)


def local(
    layer_in,
    attn_gain,
    query_weight,
    key_weight,
    value_weight,
    output_weight,
    ffn_gain,
    gate_weight,
    up_weight,
    down_weight,
    out_cotangent,
):
    bf, f32 = jnp.bfloat16, jnp.float32
    me = my_block()
    swap = [(i, BLOCKS - 1 - i) for i in range(BLOCKS)]

    def exchanged(rows):
        return lax.ppermute(rows, ("ctx", "fsdp"), swap)

    both = jnp.concatenate([layer_in, out_cotangent], 1)
    both = jnp.concatenate([both[:HALF], exchanged(both[HALF:])], 0)
    x_low, dy = both[:, :960], both[:, 960:]

    down = jnp.zeros((48, 512), bf)
    down = down.at[:40, :480].set(down_weight)
    down = down.at[40, :15].set(attn_gain).at[41, :15].set(ffn_gain)
    down = down.reshape(3, 16, 512)
    qkvo = jnp.concatenate([query_weight, key_weight, value_weight, output_weight], 1)
    mats = [jnp.pad(a, ((0, 1), (0, 0))) for a in (gate_weight, up_weight, qkvo)]
    piece = jnp.concatenate([a for i in range(3) for a in (mats[i], down[i])], 1)
    whole = gather(piece, W_DIMS, W_PARTS, "gather_weights", 1).reshape(2, 64, 16, 5376)
    flat = whole.reshape(2, 1024, 5376)
    w_gate, w_up = flat[:, :, :1280], flat[:, :, 1792:3072]
    w_qkv, w_out = flat[:, :, 3584:4384], flat[:, :, 4384:4864]
    w_down = jnp.stack([whole[..., 1280:1792], whole[..., 3072:3584], whole[..., 4864:5376]], 2)
    w_down = w_down.reshape(2, 64, 48, 512)[:, :, :40, :480].reshape(2, 2560, 480)
    gain_one = whole[0, :, 8, 4864:4880].reshape(1024).astype(f32)
    gain_two = whole[0, :, 9, 4864:4879].reshape(960).astype(f32)

    i = lax.broadcasted_iota(jnp.int32, (960, 1024), 0)
    j = lax.broadcasted_iota(jnp.int32, (960, 1024), 1)
    spread = (j == (i // 15) * 16 + i % 15).astype(bf)

    def wide(rows):
        return mm("td,de->te", rows, spread)

    def narrow_low(rows):
        return mm("te,de->td", rows, spread)

    def narrow(rows):
        high = rows.astype(bf)
        rest = rows - high.astype(f32)
        middle = rest.astype(bf)
        last = (rest - middle.astype(f32)).astype(bf)
        return narrow_low(high) + narrow_low(middle) + narrow_low(last)

    t = jnp.arange(HALF, dtype=jnp.int32)
    positions = jnp.concatenate([me * 128 + t, (BLOCKS - 1 - me) * 128 + HALF + t])
    cosine, sine = rotary_tables(positions)

    hidden = wide(x_low)
    factor_one = lax.rsqrt(jnp.sum(hidden * hidden, -1, keepdims=True) / 960 + EPS)
    normed = (hidden * factor_one * gain_one).astype(bf)
    qkv = mm("te,hec->thc", normed, w_qkv)
    query = qkv[:, :, :480].reshape(128, 960)
    key = qkv[:, :, 480:640].reshape(128, 320)
    value = qkv[:, :, 640:800].reshape(128, 320)
    query_rot = rotate(query, cosine, sine).astype(bf)
    key_rot = rotate(key, cosine, sine).astype(bf)
    kv_piece = jnp.concatenate(
        [key_rot.reshape(2, HALF, KEY_HEADS, 64), value.astype(bf).reshape(2, HALF, KEY_HEADS, 64)], -1
    ).reshape(2, HALF, 640)
    kv = gather(kv_piece, T_DIMS, T_PARTS, "gather_keys", 2).reshape(2, SIDE, 640)
    q_heads = jnp.pad(by_head(query_rot * jnp.asarray(0.125, bf)), ((0, 0), (0, 0), (0, 0), (0, 64)))
    attn_heads, lse = attend(kv, q_heads)
    attn = by_token(attn_heads)
    attn_low = attn.astype(bf)
    attn_wide = wide(attn_low).astype(bf)
    middle = x_low.astype(f32) + mm("te,hec->thc", attn_wide, w_out).reshape(128, 960)
    factor_two = lax.rsqrt(jnp.mean(middle * middle, -1, keepdims=True) + EPS)
    normed_two = wide((middle * factor_two * gain_two).astype(bf)).astype(bf)
    gate = mm("te,hec->thc", normed_two, w_gate)
    upward = mm("te,hec->thc", normed_two, w_up)
    sigma = jax.nn.sigmoid(gate)
    activated = gate * sigma
    inner = (activated * upward).astype(bf)
    inner_flat = inner.reshape(128, 2560)
    layer_out = (middle + mm("tf,hfd->thd", inner_flat, w_down).reshape(128, 960)).astype(bf)
    layer_out = jnp.concatenate([layer_out[:HALF], exchanged(layer_out[HALF:])], 0)

    dy_split = dy.reshape(128, 2, 480)
    inner_grad = mm("thd,hfd->tf", dy_split, w_down).reshape(128, 2, 1280)
    gate_low = (inner_grad * upward * sigma * (1.0 + gate * (1.0 - sigma))).astype(bf)
    up_low = (inner_grad * activated).astype(bf)
    down_term = mm("tf,thd->hfd", inner_flat, dy_split).astype(bf)
    gate_term = mm("te,thc->hec", normed_two, gate_low).astype(bf)
    up_term = mm("te,thc->hec", normed_two, up_low).astype(bf)
    grad_two = narrow(mm("thc,hec->te", gate_low, w_gate) + mm("thc,hec->te", up_low, w_up))
    weighted = gain_two * grad_two
    middle_grad = dy.astype(f32) + (
        factor_two * weighted - middle * factor_two**3 * jnp.mean(weighted * middle, -1, keepdims=True)
    )
    gain_two_term = jnp.sum(grad_two * middle * factor_two, 0)
    middle_low = middle_grad.astype(bf)
    out_term = mm("te,thd->hed", attn_wide, middle_low.reshape(128, 2, 480)).astype(bf)
    attn_grad = narrow_low(mm("thd,hed->te", middle_low.reshape(128, 2, 480), w_out).astype(bf)).astype(bf)
    delta = jnp.sum((attn_grad.astype(f32) * attn).reshape(2, HALF, KEY_HEADS, GROUPS, HEAD_SIZE), -1)
    delta = jnp.transpose(delta, (2, 0, 3, 1)).reshape(KEY_HEADS, 2, 1, LANES)
    do_heads = jnp.pad(by_head(attn_grad), ((0, 0), (0, 0), (0, 0), (64, 0)))
    dq_heads, dkv = attend_back(kv, q_heads, do_heads, lse, delta)
    dkv = dkv.reshape(2, 2, 4, 4, 2, 2, HALF, 640)
    parts = tuple(((0, c, 0),) for c in T_PARTS)
    key_sums = scatter([dkv], T_DIMS, parts, HALF, "scatter_keys", 3, VMEM_LIMIT)
    key_sums = key_sums.reshape(128, KEY_HEADS, 128)
    query_low = rotate(by_token(dq_heads) * 0.125, cosine, -sine).astype(bf)
    key_low = rotate(key_sums[..., :64].reshape(128, 320), cosine, -sine).astype(bf)
    value_low = key_sums[..., 64:].reshape(128, 320).astype(bf)
    qkv_low = jnp.concatenate(
        [query_low.reshape(128, 2, 480), key_low.reshape(128, 2, 160), value_low.reshape(128, 2, 160)], -1
    )
    qkv_term = mm("te,thc->hec", normed, qkv_low).astype(bf)
    normed_grad = mm("thc,hec->te", qkv_low, w_qkv)
    weighted = gain_one * normed_grad
    input_back = factor_one * weighted - hidden * factor_one**3 * (
        jnp.sum(weighted * hidden, -1, keepdims=True) / 960
    )
    gain_one_term = jnp.sum(normed_grad * hidden * factor_one, 0)
    input_grad = middle_grad + narrow(input_back)
    input_grad = jnp.concatenate([input_grad[:HALF], exchanged(input_grad[HALF:])], 0)

    qkvo_term = jnp.concatenate([qkv_term, out_term], -1)
    down_pad = jnp.pad(down_term.reshape(2, 64, 40, 480), ((0, 0), (0, 0), (0, 0), (0, 32)))
    gains = jnp.stack(
        [gain_one_term.reshape(64, 16)[:, :15], gain_two_term.reshape(64, 15)], 1
    ).astype(bf)
    gains = jnp.pad(gains, ((0, 0), (0, 6), (0, 512 - 15)))
    down_pad = jnp.concatenate([down_pad, jnp.broadcast_to(gains, (2, 64, 8, 512))], 2)
    down_pad = jnp.transpose(down_pad.reshape(2, 64, 3, 16, 512), (0, 1, 3, 2, 4)).reshape(2, 64, 16, 1536)
    terms = [gate_term, up_term, qkvo_term, down_pad]
    terms = [lax.optimization_barrier(a).reshape(2, 2, 4, 4, 2, 16, -1) for a in terms]
    parts = tuple(((k, (0, 1280), 0), (3, (512 * k, 512), 1280)) for k in range(3))
    sums = scatter(terms, W_DIMS, parts, 16, "scatter_weights", 4, VMEM_LIMIT)
    down_sum = jnp.concatenate([sums[:, 1280:1792], sums[:, 3072:3584], sums[:, 4864:5376]], 0)
    return (
        layer_out,
        input_grad,
        down_sum[40, :15],
        sums[:15, 3584:4064],
        sums[:15, 4064:4224],
        sums[:15, 4224:4384],
        sums[:15, 4384:4864],
        down_sum[41, :15],
        sums[:15, :1280],
        sums[:15, 1792:3072],
        down_sum[:40, :480],
    )


def solution(mesh):
    matrix, tokens = P("ctx", "fsdp"), P(("ctx", "fsdp"), None)
    return jax.shard_map(
        local,
        mesh=mesh,
        in_specs=(tokens, P("ctx"), matrix, matrix, matrix, matrix, P("ctx"), matrix, matrix, matrix, tokens),
        out_specs=(tokens, tokens, P("ctx"), matrix, matrix, matrix, matrix, P("ctx"), matrix, matrix, matrix),
        check_vma=False,
    )
```

```python
import functools

import jax
import jax.numpy as jnp
from jax import lax
from jax.experimental import pallas as pl
from jax.experimental.pallas import tpu as pltpu
from jax.sharding import PartitionSpec as P

MESH = pl.DeviceIdType.MESH
ORDERS = (("x", "y", "z"), ("y", "z", "x"), ("z", "x", "y"))
ALL = slice(None)


def whereabouts():
    ctx = lax.axis_index("ctx")
    low = lax.axis_index("fsdp")
    return {
        "x": lax.rem(lax.div(ctx, 8), 4),
        "y": lax.rem(lax.div(ctx, 2), 4),
        "z": lax.div(ctx, 32) * 2 + low,
        "c": lax.rem(ctx, 2),
    }


def device_at(at):
    ctx = ((lax.div(at["z"], 2) * 4 + at["x"]) * 4 + at["y"]) * 2 + at["c"]
    return (ctx, lax.rem(at["z"], 2))


def moved(at, axis, by):
    size = 2 if axis == "c" else 4
    return {**at, axis: lax.rem(at[axis] + by + size, size)}


def mirror():
    return (63 - lax.axis_index("ctx"), 1 - lax.axis_index("fsdp"))


def greet(me):
    barrier = pltpu.get_barrier_semaphore()
    others = [moved(me, a, s) for a in "xyz" for s in (1, -1)] + [moved(me, "c", 1)]
    targets = [device_at(other) for other in others] + [mirror()]
    for target in targets:
        pl.semaphore_signal(barrier, inc=1, device_id=target, device_id_type=MESH)
    pl.semaphore_wait(barrier, len(targets))


def start_trades(pairs, sems):
    out = []
    for k, (src, dst) in enumerate(pairs):
        half = src.shape[0] // 2
        stay = pltpu.make_async_copy(src.at[pl.ds(0, half)], dst.at[pl.ds(0, half)], sems.at[k, 0])
        go = pltpu.make_async_remote_copy(
            src_ref=src.at[pl.ds(half, half)],
            dst_ref=dst.at[pl.ds(half, half)],
            send_sem=sems.at[k, 1],
            recv_sem=sems.at[k, 2],
            device_id=mirror(),
            device_id_type=MESH,
        )
        stay.start()
        go.start()
        out += [stay, go]
    return out


def place(dims, at):
    index = []
    for d in dims:
        if d in ("zh", "zl"):
            z = at["z"]
            index.append(ALL if z is ALL else (lax.div(z, 2) if d == "zh" else lax.rem(z, 2)))
        elif d == "l":
            index.append(at.get("l", ALL))
        else:
            index.append(at[d])
    return index


def view(ref, dims, at, cols, half=None, rows=ALL):
    start, width = cols
    if half is not None:
        if "l" in dims:
            at = {**at, "l": half}
        else:
            start, width = start + half * (width // 2), width // 2
    return ref.at[tuple(place(dims, at)) + (rows, pl.ds(start, width))]


def gather_kernel(dims, parts, trades, *refs):
    piece_ref, out_ref = refs[0], refs[1 + trades]
    send, recv, sib_send, sib_recv, own_sem, trade_sem = refs[2 + 2 * trades :]
    me = whereabouts()
    greet(me)
    swaps = start_trades(list(zip(refs[1 : 1 + trades], refs[2 + trades : 2 + 2 * trades])), trade_sem)
    sibling = device_at(moved(me, "c", 1))

    def copy(src, dst, ssem, rsem, to):
        c = pltpu.make_async_remote_copy(
            src_ref=src, dst_ref=dst, send_sem=ssem, recv_sem=rsem, device_id=to, device_id_type=MESH
        )
        c.start()
        return c

    pending = []
    mine = out_ref.at[tuple(place(dims, me)) + (ALL, ALL)]
    own = pltpu.make_async_copy(piece_ref, mine, own_sem)
    own.start()
    own.wait()
    for phase in range(3):
        stage = {}
        for i, cols in enumerate(parts):
            order = ORDERS[i]
            axis = order[phase]
            base = dict(me)
            for done in order[:phase]:
                base[done] = ALL
            right, left = moved(me, axis, 1), moved(me, axis, -1)

            def blk(by, half=None, base=base, axis=axis, cols=cols):
                at = {**base, axis: lax.rem(me[axis] + by + 4, 4)}
                return view(out_ref, dims, at, cols, half)

            s, r = send.at[i, phase], recv.at[i, phase]
            to_right = copy(blk(0), blk(0), s.at[0], r.at[0], device_at(right))
            to_left = copy(blk(0), blk(0), s.at[1], r.at[1], device_at(left))
            sibs = []
            if phase == 2:
                sibs.append(copy(blk(0), blk(0), sib_send.at[i, 0], sib_recv.at[i, 0], sibling))
            stage[i] = (blk, s, r, to_right, to_left, sibs, right, left)
        for i in range(len(parts)):
            blk, s, r, to_right, to_left, sibs, right, left = stage[i]
            to_right.wait_recv()
            on_right = copy(blk(-1, 0), blk(-1, 0), s.at[2], r.at[2], device_at(right))
            if phase == 2:
                sibs.append(copy(blk(-1), blk(-1), sib_send.at[i, 1], sib_recv.at[i, 1], sibling))
            to_left.wait_recv()
            on_left = copy(blk(1, 1), blk(1, 1), s.at[3], r.at[3], device_at(left))
            if phase == 2:
                sibs.append(copy(blk(1), blk(1), sib_send.at[i, 2], sib_recv.at[i, 2], sibling))
            pending += [to_right, to_left, on_right, on_left]
            stage[i] = (blk, sibs, on_right, on_left)
        for i in range(len(parts)):
            blk, sibs, on_right, on_left = stage[i]
            on_right.wait_recv()
            on_left.wait_recv()
            if phase == 2:
                sibs.append(copy(blk(2), blk(2), sib_send.at[i, 3], sib_recv.at[i, 3], sibling))
                pending += sibs
        if phase == 2:
            for i in range(len(parts)):
                for c in stage[i][1]:
                    c.wait_recv()
    for c in pending:
        c.wait_send()
    for c in swaps:
        c.wait()


SIZE = {"zl": 2, "zh": 2, "x": 4, "y": 4, "c": 2, "l": 2}


def gather(piece, dims, parts, name, collective_id, trades=()):
    shape = tuple(SIZE[d] for d in dims) + piece.shape[-2:]
    n = len(parts)
    anywhere = pl.BlockSpec(memory_space=pl.ANY)
    return pl.pallas_call(
        functools.partial(gather_kernel, dims, parts, len(trades)),
        out_shape=(
            jax.ShapeDtypeStruct(shape, piece.dtype),
            *(jax.ShapeDtypeStruct(t.shape, t.dtype) for t in trades),
        ),
        in_specs=[anywhere] * (1 + len(trades)),
        out_specs=(anywhere,) * (1 + len(trades)),
        scratch_shapes=[
            pltpu.SemaphoreType.DMA((n, 3, 4)),
            pltpu.SemaphoreType.DMA((n, 3, 4)),
            pltpu.SemaphoreType.DMA((n, 4)),
            pltpu.SemaphoreType.DMA((n, 4)),
            pltpu.SemaphoreType.DMA,
            pltpu.SemaphoreType.DMA((max(1, len(trades)), 3)),
        ],
        compiler_params=pltpu.CompilerParams(collective_id=collective_id, has_side_effects=True),
        name=name,
    )(piece, *trades)


def scatter_kernel(dims, parts, n_in, trades, *refs):
    ins, refs = refs[:n_in], refs[n_in:]
    kept, out_ref, given, refs = refs[:trades], refs[trades], refs[trades + 1 : 2 * trades + 1], refs[2 * trades + 1 :]
    n = len(parts)
    work, sib = refs[:n], refs[n : 2 * n]
    bufs = refs[2 * n : 2 * n + 12 * n]
    load_sem, sib_send, sib_recv, send, recv, trade_sem = refs[14 * n :]
    wdims = tuple(d for d in dims if d != "c")
    me = whereabouts()
    other = moved(me, "c", 1)
    sibling = device_at(other)
    widths = [w.shape[-1] for w in work]
    starts = [sum(widths[:i]) for i in range(n)]

    def remote(src, dst, ssem, rsem, to):
        c = pltpu.make_async_remote_copy(
            src_ref=src, dst_ref=dst, send_sem=ssem, recv_sem=rsem, device_id=to, device_id_type=MESH
        )
        c.start()
        return c

    loads, pairs = {}, {}
    TURN = (2, 1, -1, 0)

    def own_loads(step):
        for i, sources in enumerate(parts):
            axis = ORDERS[i][0]
            at = {"x": ALL, "y": ALL, "z": ALL, "c": me["c"], axis: lax.rem(me[axis] + TURN[step] + 4, 4)}
            loads[i, step] = []
            for j, (k, (c0, width), d0, rows) in enumerate(sources):
                c = pltpu.make_async_copy(
                    view(ins[k], dims, at, (c0, width), None, rows),
                    view(work[i], wdims, at, (d0, width)),
                    load_sem.at[i, step, j],
                )
                c.start()
                loads[i, step].append(c)

    def sib_sends(step):
        for i, sources in enumerate(parts):
            axis = ORDERS[i][0]
            at = {"x": ALL, "y": ALL, "z": ALL, "c": other["c"], axis: lax.rem(me[axis] + TURN[step] + 4, 4)}
            pairs[i, step] = []
            for j, (k, (c0, width), d0, rows) in enumerate(sources):
                pairs[i, step].append(
                    remote(
                        view(ins[k], dims, at, (c0, width), None, rows),
                        view(sib[i], wdims, at, (d0, width)),
                        sib_send.at[i, step, j],
                        sib_recv.at[i, step, j],
                        sibling,
                    )
                )

    own_loads(0)
    greet(me)
    for step in range(4):
        sib_sends(step)
        if step:
            own_loads(step)
    swaps = start_trades(list(zip(kept, given)), trade_sem)
    pending = []

    def each_block(at, body):
        free = [d for d in wdims if (at["z"] if d in ("zh", "zl") else at.get(d, ALL)) is ALL]
        total = 1
        for d in free:
            total *= SIZE[d]

        def one(t, _):
            vals, rest = {}, t
            for d in reversed(free):
                vals[d] = lax.rem(rest, SIZE[d])
                rest = lax.div(rest, SIZE[d])
            full = []
            for d, fixed in zip(wdims, place(wdims, at)):
                full.append(vals[d] if d in vals else fixed)
            body(tuple(full), tuple(vals[d] for d in free))
            return 0

        if total == 1:
            one(jnp.int32(0), 0)
        else:
            lax.fori_loop(0, total, one, 0)

    f32 = jnp.float32

    def add(i, at, others, half=None, out=None):
        w = widths[i]
        lo, size = 0, w
        if half is not None:
            if "l" in wdims:
                at = {**at, "l": half}
            else:
                lo, size = half * (w // 2), w // 2

        def body(full, short):
            cut = (ALL, pl.ds(lo, size))
            total = work[i][full + cut].astype(f32)
            for ref, same in others:
                if same:
                    total = total + ref[full + cut].astype(f32)
                else:
                    total = total + ref[short + (ALL, ALL)].astype(f32)
            if out is None:
                work[i][full + cut] = total.astype(work[i].dtype)
            else:
                lead = (full[0],) if "l" in wdims else ()
                out[lead + (ALL, pl.ds(starts[i], w))] = total

        each_block(at, body)

    for phase in range(3):
        stage = {}

        def ctx_of(i):
            order = ORDERS[i]
            axis = order[phase]
            base = {"x": ALL, "y": ALL, "z": ALL}
            for done in order[:phase]:
                base[done] = me[done]
            return axis, base

        def at_of(i, by):
            axis, base = ctx_of(i)
            return {**base, axis: lax.rem(me[axis] + by + 4, 4)}

        def ready(i, step):
            if phase == 0:
                for c in loads[i, step]:
                    c.wait()
                for c in pairs[i, step]:
                    c.wait_recv()
                add(i, at_of(i, TURN[step]), [(sib[i], True)])

        for i in range(n):
            axis, _ = ctx_of(i)
            b = bufs[12 * i + 4 * phase : 12 * i + 4 * phase + 4]
            s, r = send.at[i, phase], recv.at[i, phase]
            ready(i, 0)
            right, left = device_at(moved(me, axis, 1)), device_at(moved(me, axis, -1))
            far = at_of(i, 2)
            one = remote(view(work[i], wdims, far, (0, widths[i]), 0), b[0], s.at[0], r.at[0], right)
            two = remote(view(work[i], wdims, far, (0, widths[i]), 1), b[1], s.at[1], r.at[1], left)
            stage[i] = [b, s, r, right, left, one, two]
        for i in range(n):
            b, s, r, right, left, one, two = stage[i]
            ready(i, 1)
            one.wait_recv()
            add(i, at_of(i, 1), [(b[0], False)], 0)
            three = remote(view(work[i], wdims, at_of(i, 1), (0, widths[i])), b[2], s.at[2], r.at[2], right)
            ready(i, 2)
            two.wait_recv()
            add(i, at_of(i, -1), [(b[1], False)], 1)
            four = remote(view(work[i], wdims, at_of(i, -1), (0, widths[i])), b[3], s.at[3], r.at[3], left)
            stage[i] = [b, three, four]
            pending += [one, two, three, four]
        for i in range(n):
            b, three, four = stage[i]
            ready(i, 3)
            three.wait_recv()
            four.wait_recv()
            add(i, at_of(i, 0), [(b[2], False), (b[3], False)], None, out_ref if phase == 2 else None)
    for c in pending:
        c.wait_send()
    for k in pairs:
        for c in pairs[k]:
            c.wait_send()
    for c in swaps:
        c.wait()


def scatter(ins, dims, parts, rows, name, collective_id, vmem, trades=()):
    n = len(parts)
    wdims = tuple(d for d in dims if d != "c")
    widths = [sum(width for _, (_, width), _, _ in sources) for sources in parts]
    wshape = tuple(SIZE[d] for d in wdims)
    dt = ins[0].dtype
    scratch = [pltpu.VMEM(wshape + (rows, w), dt) for w in widths] * 2
    for i in range(n):
        for phase in range(3):
            gone = set(ORDERS[i][: phase + 1])
            left = [d for d in wdims if ("z" if d in ("zh", "zl") else d) not in gone]
            shape = tuple(SIZE[d] for d in left)
            small = tuple(SIZE[d] for d in left if d != "l")
            halfw = widths[i] if "l" in dims else widths[i] // 2
            scratch += [pltpu.VMEM(small + (rows, halfw), dt)] * 2
            scratch += [pltpu.VMEM(shape + (rows, widths[i]), dt)] * 2
    most = max(len(s) for s in parts)
    scratch += [
        pltpu.SemaphoreType.DMA((n, 4, most)),
        pltpu.SemaphoreType.DMA((n, 4, most)),
        pltpu.SemaphoreType.DMA((n, 4, most)),
        pltpu.SemaphoreType.DMA((n, 3, 4)),
        pltpu.SemaphoreType.DMA((n, 3, 4)),
        pltpu.SemaphoreType.DMA((max(1, len(trades)), 3)),
    ]
    anywhere = pl.BlockSpec(memory_space=pl.ANY)
    lead = (2,) if "l" in dims else ()
    return pl.pallas_call(
        functools.partial(scatter_kernel, dims, parts, len(ins), len(trades)),
        out_shape=(
            jax.ShapeDtypeStruct(lead + (rows, sum(widths)), jnp.float32),
            *(jax.ShapeDtypeStruct(t.shape, t.dtype) for t in trades),
        ),
        in_specs=[anywhere] * (len(ins) + len(trades)),
        out_specs=(pl.BlockSpec(memory_space=pltpu.VMEM),) + (anywhere,) * len(trades),
        scratch_shapes=scratch,
        compiler_params=pltpu.CompilerParams(
            collective_id=collective_id, has_side_effects=True, vmem_limit_bytes=vmem
        ),
        name=name,
    )(*ins, *trades)


W_DIMS = ("zl", "zh", "x", "y", "c")
W_PARTS = ((0, 1792), (1792, 1792), (3584, 1792))
T_DIMS = ("l", "zh", "x", "y", "c", "zl")
T_PARTS = ((0, 256), (256, 256), (512, 128))


QH = 15
KEY_HEADS = 5
GROUPS = 3
HEAD_SIZE = 64
EPS = 1e-05
ROPE_BASE = 10000.0
NEGATIVE = -1e30
LOG2E = 1.4426950408889634
BLOCKS = 128
HALF = 64
SIDE = BLOCKS * HALF
LANES = GROUPS * HALF
CHUNK = 512
UNROLL = 2
VMEM_LIMIT = 56 << 20


def chunk_ranges(side, own):
    count = SIDE // CHUNK
    if side == 0:
        diag = lax.div(HALF * own, CHUNK)
        first = HALF * (BLOCKS - own)
        edge, whole = lax.div(first, CHUNK), lax.div(first + CHUNK - 1, CHUNK)
        return ((diag, diag + 1), (0, diag)), ((edge, whole), (whole, count))
    rows = HALF * (own + 1)
    edge, whole = lax.div(rows, CHUNK), lax.div(rows + CHUNK - 1, CHUNK)
    diag = lax.div(HALF * (BLOCKS - 1 - own), CHUNK)
    return ((edge, whole), (0, edge)), ((diag, diag + 1), (diag + 1, count))


def seen(source, chunk, side, own):
    row = chunk * CHUNK + lax.broadcasted_iota(jnp.int32, (CHUNK, LANES), 0)
    block, place = row // HALF, row % HALF
    if source == 0:
        key = block * (2 * HALF) + place
    else:
        key = (BLOCKS - 1 - block) * (2 * HALF) + HALF + place
    col = lax.broadcasted_iota(jnp.int32, (CHUNK, LANES), 1)
    return key <= own * (2 * HALF) + side * HALF + col % HALF


def dot_nt(a, b):
    return lax.dot_general(a, b, (((1,), (1,)), ((), ())), preferred_element_type=jnp.float32)


def dot_tn(a, b):
    return lax.dot_general(a, b, (((0,), (0,)), ((), ())), preferred_element_type=jnp.float32)


def dot_nn(a, b):
    return lax.dot_general(a, b, (((1,), (0,)), ((), ())), preferred_element_type=jnp.float32)


def my_block():
    return lax.axis_index("ctx") * 2 + lax.axis_index("fsdp")


def attend_kernel(kv_ref, q_ref, o_ref, lse_ref, *acc_refs):
    me = my_block()
    for side in range(2):
        own = me if side == 0 else BLOCKS - 1 - me
        q = q_ref[0, side]
        for acc in acc_refs:
            acc[...] = jnp.zeros_like(acc)
        low = jnp.full((1, LANES), NEGATIVE, jnp.float32)
        none = jnp.zeros((1, LANES), jnp.float32)

        def step(source, masked, width, first, chunk, carry):
            out = []
            for u in range(width):
                peak, total = carry[u]
                at = first + (chunk - first) * width + u
                kv = kv_ref[source, pl.ds(pl.multiple_of(at * CHUNK, CHUNK), CHUNK), :]
                s = dot_nt(kv, q) * LOG2E
                if masked:
                    s = jnp.where(seen(source, at, side, own), s, NEGATIVE)
                new = jnp.maximum(peak, jnp.max(s, 0, keepdims=True))
                p = jnp.exp2(s - new)
                scale = jnp.exp2(peak - new)
                total = total * scale + jnp.sum(p, 0, keepdims=True)
                acc_refs[u][...] = acc_refs[u][...] * scale + dot_tn(kv, p.astype(jnp.bfloat16))
                out.append((new, total))
            return tuple(out) + tuple(carry[width:])

        carry = ((low, none),) * len(acc_refs)
        for source, (edge, whole) in enumerate(chunk_ranges(side, own)):
            carry = lax.fori_loop(edge[0], edge[1], functools.partial(step, source, True, 1, edge[0]), carry)
            start, end = whole
            for width in (UNROLL, 1):
                count = lax.div(end - start, width)
                carry = lax.fori_loop(
                    start, start + count, functools.partial(step, source, False, width, start), carry
                )
                start = start + count * width
        peak = functools.reduce(jnp.maximum, [c[0] for c in carry])
        total, out = none, 0.0
        for (top, part), acc in zip(carry, acc_refs):
            scale = jnp.exp2(top - peak)
            total = total + part * scale
            out = out + acc[HEAD_SIZE:, :] * scale
        o_ref[0, side] = out / total
        lse_ref[0, side] = peak + jnp.log2(total)


def attend(kv, q):
    return pl.pallas_call(
        attend_kernel,
        grid=(KEY_HEADS,),
        out_shape=(
            jax.ShapeDtypeStruct((KEY_HEADS, 2, HEAD_SIZE, LANES), jnp.float32),
            jax.ShapeDtypeStruct((KEY_HEADS, 2, 1, LANES), jnp.float32),
        ),
        in_specs=[
            pl.BlockSpec((2, SIDE, 128), lambda h: (0, 0, h)),
            pl.BlockSpec((1, 2, LANES, 128), lambda h: (h, 0, 0, 0)),
        ],
        out_specs=(
            pl.BlockSpec((1, 2, HEAD_SIZE, LANES), lambda h: (h, 0, 0, 0)),
            pl.BlockSpec((1, 2, 1, LANES), lambda h: (h, 0, 0, 0)),
        ),
        scratch_shapes=[pltpu.VMEM((128, LANES), jnp.float32)] * UNROLL,
        compiler_params=pltpu.CompilerParams(vmem_limit_bytes=VMEM_LIMIT),
        name="attend",
    )(kv, q)


def attend_back_kernel(kv_ref, q_ref, do_ref, lse_ref, delta_ref, dq_ref, dkv_ref, acc_ref):
    me = my_block()
    dkv_ref[...] = jnp.zeros_like(dkv_ref)
    for side in range(2):
        own = me if side == 0 else BLOCKS - 1 - me
        q, do = q_ref[0, side], do_ref[0, side]
        lse, delta = lse_ref[0, side], delta_ref[0, side]
        acc_ref[...] = jnp.zeros_like(acc_ref)

        def step(source, masked, width, first, chunk, carry):
            dq = 0.0
            for u in range(width):
                at = first + (chunk - first) * width + u
                rows = pl.ds(pl.multiple_of(at * CHUNK, CHUNK), CHUNK)
                kv = kv_ref[source, rows, :]
                p = jnp.exp2(dot_nt(kv, q) * LOG2E - lse)
                if masked:
                    p = jnp.where(seen(source, at, side, own), p, 0.0)
                ds = (p * (dot_nt(kv, do) - delta)).astype(jnp.bfloat16)
                more = dot_nn(ds, q) + dot_nn(p.astype(jnp.bfloat16), do)
                dkv_ref[source, rows, :] = (dkv_ref[source, rows, :].astype(jnp.float32) + more).astype(jnp.bfloat16)
                dq = dq + dot_tn(kv, ds)
            acc_ref[...] += dq
            return carry

        for source, (edge, whole) in enumerate(chunk_ranges(side, own)):
            lax.fori_loop(edge[0], edge[1], functools.partial(step, source, True, 1, edge[0]), 0)
            start, end = whole
            for width in (UNROLL, 1):
                count = lax.div(end - start, width)
                lax.fori_loop(start, start + count, functools.partial(step, source, False, width, start), 0)
                start = start + count * width
        dq_ref[0, side] = acc_ref[:HEAD_SIZE, :]


def attend_back(kv, q, do, lse, delta):
    per_head = pl.BlockSpec((1, 2, LANES, 128), lambda h: (h, 0, 0, 0))
    row = pl.BlockSpec((1, 2, 1, LANES), lambda h: (h, 0, 0, 0))
    keys = pl.BlockSpec((2, SIDE, 128), lambda h: (0, 0, h))
    return pl.pallas_call(
        attend_back_kernel,
        grid=(KEY_HEADS,),
        out_shape=(
            jax.ShapeDtypeStruct((KEY_HEADS, 2, HEAD_SIZE, LANES), jnp.float32),
            jax.ShapeDtypeStruct(kv.shape, jnp.bfloat16),
        ),
        in_specs=[keys, per_head, per_head, row, row],
        out_specs=(pl.BlockSpec((1, 2, HEAD_SIZE, LANES), lambda h: (h, 0, 0, 0)), keys),
        scratch_shapes=[pltpu.VMEM((128, LANES), jnp.float32)],
        compiler_params=pltpu.CompilerParams(vmem_limit_bytes=VMEM_LIMIT),
        name="attend_back",
    )(kv, q, do, lse, delta)


def rotary_tables(positions):
    half = HEAD_SIZE // 2
    freq = ROPE_BASE ** (-(jnp.arange(half, dtype=jnp.float32) * 2.0 / HEAD_SIZE))
    angle = positions.astype(jnp.float32)[:, None] * freq[None, :]
    return (jnp.cos(angle)[:, None, :], jnp.sin(angle)[:, None, :])


def rotate(values, cosine, sine):
    count = values.shape[0]
    half = HEAD_SIZE // 2
    heads = values.reshape(count, -1, HEAD_SIZE)
    first = heads[..., :half]
    second = heads[..., half:]
    return jnp.concatenate(
        [first * cosine - second * sine, second * cosine + first * sine], -1
    ).reshape(count, -1)


def mm(form, left, right):
    return jnp.einsum(form, left, right, preferred_element_type=jnp.float32)


def by_head(rows):
    r = rows.reshape(2, HALF, KEY_HEADS, GROUPS, HEAD_SIZE)
    return jnp.transpose(r, (2, 0, 3, 1, 4)).reshape(KEY_HEADS, 2, LANES, HEAD_SIZE)


def by_token(heads):
    h = heads.reshape(KEY_HEADS, 2, HEAD_SIZE, GROUPS, HALF)
    return jnp.transpose(h, (1, 4, 0, 3, 2)).reshape(2 * HALF, QH * HEAD_SIZE)


def outer_kernel(left_ref, right_ref, out_ref):
    out_ref[0] = dot_tn(left_ref[...], right_ref[0]).astype(jnp.bfloat16)


def outer(left, right, steps):
    tokens, m = left.shape
    n = right.shape[-1]
    return pl.pallas_call(
        outer_kernel,
        grid=(2, steps),
        out_shape=jax.ShapeDtypeStruct((2, m, n), jnp.bfloat16),
        in_specs=[
            pl.BlockSpec((tokens, m // steps), lambda h, s: (0, s)),
            pl.BlockSpec((1, tokens, n), lambda h, s: (h, 0, 0)),
        ],
        out_specs=pl.BlockSpec((1, m // steps, n), lambda h, s: (h, s, 0)),
        compiler_params=pltpu.CompilerParams(vmem_limit_bytes=VMEM_LIMIT),
        name="outer",
    )(left, right)


def thirds(rows):
    high = rows.astype(jnp.bfloat16)
    rest = rows - high.astype(jnp.float32)
    middle = rest.astype(jnp.bfloat16)
    return high, middle, (rest - middle.astype(jnp.float32)).astype(jnp.bfloat16)


def ffn_kernel(
    whole_ref, attn_ref, x_ref, dy_ref, gain_ref, spread_ref, spread_down_ref,
    layer_out_ref, middle_grad_ref, attn_grad_ref, attn_wide_ref, normed_ref, gate_low_ref, up_low_ref,
    inner_ref, middle_low_ref, gain_grad_ref,
    w_out, w_gate, w_up, w_down, gate_s, up_s, sems,
):
    bf, f32 = jnp.bfloat16, jnp.float32

    def fetch(dst, start, width, sem):
        c = pltpu.make_async_copy(whole_ref.at[:, :, :, pl.ds(start, width)], dst, sem)
        c.start()
        return c

    get_out = fetch(w_out, 3584, 512, sems.at[0])
    get_gate = fetch(w_gate, 0, 1280, sems.at[1])
    get_up = fetch(w_up, 1792, 1280, sems.at[2])
    get_down = [
        fetch(w_down.at[:, :, pl.ds(16 * g, 16), :], 1280 + 1792 * g, 512, sems.at[3 + g]) for g in range(3)
    ]
    real = lax.broadcasted_iota(jnp.int32, (128, 512), 1) < 480

    attn_wide = 0.0
    for h in range(2):
        attn_wide = attn_wide + dot_nn(attn_ref[h].astype(bf), spread_ref[h])
    attn_wide = attn_wide.astype(bf)
    attn_wide_ref[...] = attn_wide
    get_out.wait()
    middle, squares = [], 0.0
    for h in range(2):
        part = dot_nn(attn_wide, w_out[h].reshape(1024, 512))
        part = x_ref[h].astype(f32) + jnp.where(real, part, 0.0)
        squares = squares + jnp.sum(part * part, -1, keepdims=True)
        middle.append(part)
    factor = lax.rsqrt(squares / 960 + EPS)
    normed = 0.0
    for h in range(2):
        normed = normed + dot_nn((middle[h] * factor * gain_ref[h]).astype(bf), spread_ref[h])
    normed = normed.astype(bf)
    normed_ref[...] = normed
    get_gate.wait()
    get_up.wait()
    for h in range(2):
        gate = dot_nn(normed, w_gate[h].reshape(1024, 1280))
        up = dot_nn(normed, w_up[h].reshape(1024, 1280))
        gate_s[h], up_s[h] = gate, up
        inner = (gate * jax.nn.sigmoid(gate) * up).astype(bf)
        for b in range(2):
            inner_ref[:, pl.ds(768 * (2 * h + b), 768)] = dot_nn(
                inner[:, 640 * b : 640 * b + 640], spread_down_ref[...]
            ).astype(bf)
    for c in get_down:
        c.wait()
    for h in range(2):
        low = dot_nn(inner_ref[...], w_down[h].reshape(3072, 512))
        layer_out_ref[h] = (middle[h] + low).astype(bf)
    normed_grad = 0.0
    for h in range(2):
        for b in range(2):
            blocks = pl.ds(16 * (2 * h + b), 16)
            wide_grad = 0.0
            for d in range(2):
                wide_grad = wide_grad + dot_nt(dy_ref[d], w_down[d, blocks].reshape(768, 512))
            inner_grad = 0.0
            for t in thirds(wide_grad):
                inner_grad = inner_grad + dot_nt(t, spread_down_ref[...])
            cols = pl.ds(640 * b, 640)
            gate, up = gate_s[h, :, cols], up_s[h, :, cols]
            sigma = jax.nn.sigmoid(gate)
            gate_low_ref[h, :, cols] = (inner_grad * up * sigma * (1.0 + gate * (1.0 - sigma))).astype(bf)
            up_low_ref[h, :, cols] = (inner_grad * (gate * sigma)).astype(bf)
        normed_grad = normed_grad + dot_nt(gate_low_ref[h], w_gate[h].reshape(1024, 1280))
        normed_grad = normed_grad + dot_nt(up_low_ref[h], w_up[h].reshape(1024, 1280))
    split = thirds(normed_grad)
    grads, mean = [], 0.0
    for h in range(2):
        g = 0.0
        for t in split:
            g = g + dot_nt(t, spread_ref[h])
        gain_grad_ref[h] = jnp.sum(g * middle[h] * factor, 0, keepdims=True)
        g = g * gain_ref[h]
        mean = mean + jnp.sum(g * middle[h], -1, keepdims=True)
        grads.append(g)
    wide_grad = 0.0
    for h in range(2):
        total = dy_ref[h].astype(f32) + factor * grads[h] - middle[h] * (factor * factor * factor * (mean / 960))
        middle_grad_ref[h] = total
        middle_low_ref[h] = total.astype(bf)
        wide_grad = wide_grad + dot_nt(total.astype(bf), w_out[h].reshape(1024, 512))
    wide_grad = wide_grad.astype(bf)
    for h in range(2):
        attn_grad_ref[h] = dot_nt(wide_grad, spread_ref[h]).astype(bf)


def ffn(whole, attn, x, dy, gain, spread, spread_down):
    bf, f32 = jnp.bfloat16, jnp.float32
    vmem = pl.BlockSpec(memory_space=pltpu.VMEM)
    shapes = [
        ((2, 128, 512), bf), ((2, 128, 512), f32), ((2, 128, 512), bf), ((128, 1024), bf), ((128, 1024), bf),
        ((2, 128, 1280), bf), ((2, 128, 1280), bf), ((128, 3072), bf), ((2, 128, 512), bf), ((2, 1, 512), f32),
    ]
    return pl.pallas_call(
        ffn_kernel,
        out_shape=tuple(jax.ShapeDtypeStruct(s, d) for s, d in shapes),
        in_specs=[pl.BlockSpec(memory_space=pl.ANY)] + [vmem] * 6,
        out_specs=(vmem,) * len(shapes),
        scratch_shapes=[
            pltpu.VMEM((2, 64, 16, 512), bf),
            pltpu.VMEM((2, 64, 16, 1280), bf),
            pltpu.VMEM((2, 64, 16, 1280), bf),
            pltpu.VMEM((2, 64, 48, 512), bf),
            pltpu.VMEM((2, 128, 1280), f32),
            pltpu.VMEM((2, 128, 1280), f32),
            pltpu.SemaphoreType.DMA((6,)),
        ],
        compiler_params=pltpu.CompilerParams(vmem_limit_bytes=VMEM_LIMIT),
        name="ffn",
    )(whole, attn, x, dy, gain, spread, spread_down)


def halves(rows):
    both = jnp.stack([rows[:, :480], rows[:, 480:]])
    return jnp.pad(both, ((0, 0), (0, 0), (0, 32)))


def joined(both):
    return jnp.concatenate([both[0, :, :480], both[1, :, :480]], 1)


def local(
    layer_in,
    attn_gain,
    query_weight,
    key_weight,
    value_weight,
    output_weight,
    ffn_gain,
    gate_weight,
    up_weight,
    down_weight,
    out_cotangent,
):
    bf, f32 = jnp.bfloat16, jnp.float32
    me = my_block()

    down = jnp.zeros((48, 512), bf)
    down = down.at[:40, :480].set(down_weight)
    down = down.at[40, :15].set(attn_gain).at[41, :15].set(ffn_gain)
    down = down.reshape(3, 16, 512)
    oqkv = jnp.concatenate([output_weight, query_weight, key_weight, value_weight], 1)
    mats = [jnp.pad(a, ((0, 1), (0, 0))) for a in (gate_weight, up_weight, oqkv)]
    piece = jnp.concatenate([a for i in range(3) for a in (mats[i], down[i])], 1)
    whole, x_low, dy = gather(piece, W_DIMS, W_PARTS, "gather_weights", 1, (layer_in, out_cotangent))
    whole = whole.reshape(2, 64, 16, 5376)
    w_qkv = whole.reshape(2, 1024, 5376)[:, :, 4064:4864]
    gain_one = whole[0, :, 8, 4864:4880].reshape(1024).astype(f32)
    gain_two = whole[0, :, 9, 4864:4879].reshape(1, 960).astype(f32)

    i = lax.broadcasted_iota(jnp.int32, (2, 512, 1024), 1)
    d = i + 480 * lax.broadcasted_iota(jnp.int32, (2, 512, 1024), 0)
    j = lax.broadcasted_iota(jnp.int32, (2, 512, 1024), 2)
    spread = jnp.logical_and(i < 480, j == (d // 15) * 16 + d % 15).astype(bf)
    i = lax.broadcasted_iota(jnp.int32, (640, 768), 0)
    j = lax.broadcasted_iota(jnp.int32, (640, 768), 1)
    spread_down = (j == (i // 40) * 48 + i % 40).astype(bf)

    t = jnp.arange(HALF, dtype=jnp.int32)
    positions = jnp.concatenate([me * 128 + t, (BLOCKS - 1 - me) * 128 + HALF + t])
    cosine, sine = rotary_tables(positions)

    x_halves, dy_halves = halves(x_low), halves(dy)
    hidden = mm("htd,hde->te", x_halves, spread)
    factor_one = lax.rsqrt(jnp.sum(hidden * hidden, -1, keepdims=True) / 960 + EPS)
    normed = (hidden * factor_one * gain_one).astype(bf)
    qkv = mm("te,hec->thc", normed, w_qkv)
    query = qkv[:, :, :480].reshape(128, 960)
    key = qkv[:, :, 480:640].reshape(128, 320)
    value = qkv[:, :, 640:800].reshape(128, 320)
    query_rot = rotate(query, cosine, sine).astype(bf)
    key_rot = rotate(key, cosine, sine).astype(bf)
    kv_piece = jnp.concatenate(
        [key_rot.reshape(2, HALF, KEY_HEADS, 64), value.astype(bf).reshape(2, HALF, KEY_HEADS, 64)], -1
    ).reshape(2, HALF, 640)
    (kv,) = gather(kv_piece, T_DIMS, T_PARTS, "gather_keys", 2)
    kv = kv.reshape(2, SIDE, 640)
    q_heads = jnp.pad(by_head(query_rot * jnp.asarray(0.125, bf)), ((0, 0), (0, 0), (0, 0), (0, 64)))
    attn_heads, lse = attend(kv, q_heads)
    attn = by_token(attn_heads)
    (layer_out, middle_grad, attn_grad, attn_wide, normed_two, gate_low, up_low, inner, middle_low, gain_two_term) = ffn(
        whole, halves(attn), x_halves, dy_halves, halves(gain_two), spread, spread_down
    )
    layer_out, middle_grad, attn_grad = joined(layer_out), joined(middle_grad), joined(attn_grad)
    delta = jnp.sum((attn_grad.astype(f32) * attn).reshape(2, HALF, KEY_HEADS, GROUPS, HEAD_SIZE), -1)
    delta = jnp.transpose(delta, (2, 0, 3, 1)).reshape(KEY_HEADS, 2, 1, LANES)
    do_heads = jnp.pad(by_head(attn_grad), ((0, 0), (0, 0), (0, 0), (64, 0)))
    dq_heads, dkv = attend_back(kv, q_heads, do_heads, lse, delta)
    dkv = dkv.reshape(2, 2, 4, 4, 2, 2, HALF, 640)
    parts = tuple(((0, c, 0, ALL),) for c in T_PARTS)
    key_sums, layer_out = scatter([dkv], T_DIMS, parts, HALF, "scatter_keys", 3, VMEM_LIMIT, (layer_out,))
    key_sums = key_sums.reshape(128, KEY_HEADS, 128)
    query_low = rotate(by_token(dq_heads) * 0.125, cosine, -sine).astype(bf)
    key_low = rotate(key_sums[..., :64].reshape(128, 320), cosine, -sine).astype(bf)
    value_low = key_sums[..., 64:].reshape(128, 320).astype(bf)
    qkv_low = jnp.concatenate(
        [query_low.reshape(128, 2, 480), key_low.reshape(128, 2, 160), value_low.reshape(128, 2, 160)], -1
    )
    normed_grad = mm("thc,hec->te", qkv_low, w_qkv)
    weighted = gain_one * normed_grad
    input_back = factor_one * weighted - hidden * factor_one**3 * (
        jnp.sum(weighted * hidden, -1, keepdims=True) / 960
    )
    gain_one_term = jnp.sum(normed_grad * hidden * factor_one, 0)
    input_back = sum(mm("te,hde->htd", part, spread) for part in thirds(input_back))
    input_grad = middle_grad + joined(input_back)

    gains = jnp.concatenate([gain_one_term.reshape(64, 16)[:, :15], joined(gain_two_term).reshape(64, 15)], 1)
    gains = jnp.pad(gains.astype(bf), ((0, 0), (0, 1280 - 30)))
    right = jnp.concatenate(
        [
            jnp.pad(jnp.transpose(qkv_low, (1, 0, 2)), ((0, 0), (0, 0), (480, 0))),
            jnp.pad(middle_low[:, :, :480], ((0, 0), (0, 0), (0, 800))),
            jnp.stack([gains, gains]),
        ],
        1,
    )
    slot = lax.broadcasted_iota(jnp.int32, (64, 1024), 0) * 16 + 15
    slot = (slot == lax.broadcasted_iota(jnp.int32, (64, 1024), 1)).astype(bf)
    left = jnp.concatenate([normed, attn_wide, slot], 0)
    terms = [outer(normed_two, gate_low, 2), outer(normed_two, up_low, 2), outer(left, right, 2)]
    terms = [a.reshape(2, 2, 4, 4, 2, 16, 1280) for a in terms]
    terms.append(outer(inner, dy_halves, 3).reshape(2, 2, 4, 4, 2, 48, 512))
    parts = tuple(((k, (0, 1280), 0, ALL), (3, (0, 512), 1280, pl.ds(16 * k, 16))) for k in range(3))
    sums, input_grad = scatter(terms, W_DIMS, parts, 16, "scatter_weights", 4, VMEM_LIMIT, (input_grad,))
    down_sum = jnp.concatenate([sums[:, 1280:1792], sums[:, 3072:3584], sums[:, 4864:5376]], 0)
    return (
        layer_out,
        input_grad,
        sums[15, 3584:3599],
        sums[:15, 4064:4544],
        sums[:15, 4544:4704],
        sums[:15, 4704:4864],
        sums[:15, 3584:4064],
        sums[15, 3599:3614],
        sums[:15, :1280],
        sums[:15, 1792:3072],
        down_sum[:40, :480],
    )


def solution(mesh):
    matrix, tokens = P("ctx", "fsdp"), P(("ctx", "fsdp"), None)
    return jax.shard_map(
        local,
        mesh=mesh,
        in_specs=(tokens, P("ctx"), matrix, matrix, matrix, matrix, P("ctx"), matrix, matrix, matrix, tokens),
        out_specs=(tokens, tokens, P("ctx"), matrix, matrix, matrix, matrix, P("ctx"), matrix, matrix, matrix),
        check_vma=False,
    )
```

```python
import functools

import jax
import jax.numpy as jnp
from jax import lax
from jax.experimental import pallas as pl
from jax.experimental.pallas import tpu as pltpu
from jax.sharding import PartitionSpec as P

MESH = pl.DeviceIdType.MESH
ORDERS = (("x", "y", "z"), ("y", "z", "x"), ("z", "x", "y"))
ALL = slice(None)


def whereabouts():
    ctx = lax.axis_index("ctx")
    low = lax.axis_index("fsdp")
    return {
        "x": lax.rem(lax.div(ctx, 8), 4),
        "y": lax.rem(lax.div(ctx, 2), 4),
        "z": lax.div(ctx, 32) * 2 + low,
        "c": lax.rem(ctx, 2),
    }


def device_at(at):
    ctx = ((lax.div(at["z"], 2) * 4 + at["x"]) * 4 + at["y"]) * 2 + at["c"]
    return (ctx, lax.rem(at["z"], 2))


def moved(at, axis, by):
    size = 2 if axis == "c" else 4
    return {**at, axis: lax.rem(at[axis] + by + size, size)}


def mirror():
    return (63 - lax.axis_index("ctx"), 1 - lax.axis_index("fsdp"))


def greet(me):
    barrier = pltpu.get_barrier_semaphore()
    others = [moved(me, a, s) for a in "xyz" for s in (1, -1)] + [moved(me, "c", 1)]
    targets = [device_at(other) for other in others] + [mirror()]
    for target in targets:
        pl.semaphore_signal(barrier, inc=1, device_id=target, device_id_type=MESH)
    pl.semaphore_wait(barrier, len(targets))


def start_trades(pairs, sems):
    out = []
    for k, (src, dst) in enumerate(pairs):
        half = src.shape[0] // 2
        stay = pltpu.make_async_copy(src.at[pl.ds(0, half)], dst.at[pl.ds(0, half)], sems.at[k, 0])
        go = pltpu.make_async_remote_copy(
            src_ref=src.at[pl.ds(half, half)],
            dst_ref=dst.at[pl.ds(half, half)],
            send_sem=sems.at[k, 1],
            recv_sem=sems.at[k, 2],
            device_id=mirror(),
            device_id_type=MESH,
        )
        stay.start()
        go.start()
        out += [stay, go]
    return out


def place(dims, at):
    index = []
    for d in dims:
        if d in ("zh", "zl"):
            z = at["z"]
            index.append(ALL if z is ALL else (lax.div(z, 2) if d == "zh" else lax.rem(z, 2)))
        elif d == "l":
            index.append(at.get("l", ALL))
        else:
            index.append(at[d])
    return index


def view(ref, dims, at, cols, half=None, rows=ALL):
    start, width = cols
    if half is not None:
        if "l" in dims:
            at = {**at, "l": half}
        else:
            start, width = start + half * (width // 2), width // 2
    return ref.at[tuple(place(dims, at)) + (rows, pl.ds(start, width))]


def gather_kernel(dims, parts, trades, *refs):
    piece_ref, out_ref = refs[0], refs[1 + trades]
    send, recv, sib_send, sib_recv, own_sem, trade_sem = refs[2 + 2 * trades :]
    me = whereabouts()
    greet(me)
    swaps = start_trades(list(zip(refs[1 : 1 + trades], refs[2 + trades : 2 + 2 * trades])), trade_sem)
    sibling = device_at(moved(me, "c", 1))

    def copy(src, dst, ssem, rsem, to):
        c = pltpu.make_async_remote_copy(
            src_ref=src, dst_ref=dst, send_sem=ssem, recv_sem=rsem, device_id=to, device_id_type=MESH
        )
        c.start()
        return c

    pending = []
    mine = out_ref.at[tuple(place(dims, me)) + (ALL, ALL)]
    own = pltpu.make_async_copy(piece_ref, mine, own_sem)
    own.start()
    own.wait()
    for phase in range(3):
        stage = {}
        for i, cols in enumerate(parts):
            order = ORDERS[i]
            axis = order[phase]
            base = dict(me)
            for done in order[:phase]:
                base[done] = ALL
            right, left = moved(me, axis, 1), moved(me, axis, -1)

            def blk(by, half=None, base=base, axis=axis, cols=cols):
                at = {**base, axis: lax.rem(me[axis] + by + 4, 4)}
                return view(out_ref, dims, at, cols, half)

            s, r = send.at[i, phase], recv.at[i, phase]
            to_right = copy(blk(0), blk(0), s.at[0], r.at[0], device_at(right))
            to_left = copy(blk(0), blk(0), s.at[1], r.at[1], device_at(left))
            sibs = []
            if phase == 2:
                sibs.append(copy(blk(0), blk(0), sib_send.at[i, 0], sib_recv.at[i, 0], sibling))
            stage[i] = (blk, s, r, to_right, to_left, sibs, right, left)
        for i in range(len(parts)):
            blk, s, r, to_right, to_left, sibs, right, left = stage[i]
            to_right.wait_recv()
            on_right = copy(blk(-1, 0), blk(-1, 0), s.at[2], r.at[2], device_at(right))
            if phase == 2:
                sibs.append(copy(blk(-1), blk(-1), sib_send.at[i, 1], sib_recv.at[i, 1], sibling))
            to_left.wait_recv()
            on_left = copy(blk(1, 1), blk(1, 1), s.at[3], r.at[3], device_at(left))
            if phase == 2:
                sibs.append(copy(blk(1), blk(1), sib_send.at[i, 2], sib_recv.at[i, 2], sibling))
            pending += [to_right, to_left, on_right, on_left]
            stage[i] = (blk, sibs, on_right, on_left)
        for i in range(len(parts)):
            blk, sibs, on_right, on_left = stage[i]
            on_right.wait_recv()
            on_left.wait_recv()
            if phase == 2:
                sibs.append(copy(blk(2), blk(2), sib_send.at[i, 3], sib_recv.at[i, 3], sibling))
                pending += sibs
        if phase == 2:
            for i in range(len(parts)):
                for c in stage[i][1]:
                    c.wait_recv()
    for c in pending:
        c.wait_send()
    for c in swaps:
        c.wait()


SIZE = {"zl": 2, "zh": 2, "x": 4, "y": 4, "c": 2, "l": 2}


def gather(piece, dims, parts, name, collective_id, trades=()):
    shape = tuple(SIZE[d] for d in dims) + piece.shape[-2:]
    n = len(parts)
    anywhere = pl.BlockSpec(memory_space=pl.ANY)
    return pl.pallas_call(
        functools.partial(gather_kernel, dims, parts, len(trades)),
        out_shape=(
            jax.ShapeDtypeStruct(shape, piece.dtype),
            *(jax.ShapeDtypeStruct(t.shape, t.dtype) for t in trades),
        ),
        in_specs=[anywhere] * (1 + len(trades)),
        out_specs=(anywhere,) * (1 + len(trades)),
        scratch_shapes=[
            pltpu.SemaphoreType.DMA((n, 3, 4)),
            pltpu.SemaphoreType.DMA((n, 3, 4)),
            pltpu.SemaphoreType.DMA((n, 4)),
            pltpu.SemaphoreType.DMA((n, 4)),
            pltpu.SemaphoreType.DMA,
            pltpu.SemaphoreType.DMA((max(1, len(trades)), 3)),
        ],
        compiler_params=pltpu.CompilerParams(collective_id=collective_id, has_side_effects=True),
        name=name,
    )(piece, *trades)


def scatter_kernel(dims, parts, n_in, trades, *refs):
    ins, refs = refs[:n_in], refs[n_in:]
    kept, out_ref, given, refs = refs[:trades], refs[trades], refs[trades + 1 : 2 * trades + 1], refs[2 * trades + 1 :]
    n = len(parts)
    work, sib = refs[:n], refs[n : 2 * n]
    bufs = refs[2 * n : 2 * n + 12 * n]
    load_sem, sib_send, sib_recv, send, recv, trade_sem = refs[14 * n :]
    wdims = tuple(d for d in dims if d != "c")
    me = whereabouts()
    other = moved(me, "c", 1)
    sibling = device_at(other)
    widths = [w.shape[-1] for w in work]
    starts = [sum(widths[:i]) for i in range(n)]

    def remote(src, dst, ssem, rsem, to):
        c = pltpu.make_async_remote_copy(
            src_ref=src, dst_ref=dst, send_sem=ssem, recv_sem=rsem, device_id=to, device_id_type=MESH
        )
        c.start()
        return c

    loads, pairs = {}, {}
    TURN = (2, 1, -1, 0)

    def own_loads(step):
        for i, sources in enumerate(parts):
            axis = ORDERS[i][0]
            at = {"x": ALL, "y": ALL, "z": ALL, "c": me["c"], axis: lax.rem(me[axis] + TURN[step] + 4, 4)}
            loads[i, step] = []
            for j, (k, (c0, width), d0, rows) in enumerate(sources):
                c = pltpu.make_async_copy(
                    view(ins[k], dims, at, (c0, width), None, rows),
                    view(work[i], wdims, at, (d0, width)),
                    load_sem.at[i, step, j],
                )
                c.start()
                loads[i, step].append(c)

    def sib_sends(step):
        for i, sources in enumerate(parts):
            axis = ORDERS[i][0]
            at = {"x": ALL, "y": ALL, "z": ALL, "c": other["c"], axis: lax.rem(me[axis] + TURN[step] + 4, 4)}
            pairs[i, step] = []
            for j, (k, (c0, width), d0, rows) in enumerate(sources):
                pairs[i, step].append(
                    remote(
                        view(ins[k], dims, at, (c0, width), None, rows),
                        view(sib[i], wdims, at, (d0, width)),
                        sib_send.at[i, step, j],
                        sib_recv.at[i, step, j],
                        sibling,
                    )
                )

    own_loads(0)
    greet(me)
    for step in range(4):
        sib_sends(step)
        if step:
            own_loads(step)
    swaps = start_trades(list(zip(kept, given)), trade_sem)
    pending = []

    def each_block(at, body):
        free = [d for d in wdims if (at["z"] if d in ("zh", "zl") else at.get(d, ALL)) is ALL]
        total = 1
        for d in free:
            total *= SIZE[d]

        def one(t, _):
            vals, rest = {}, t
            for d in reversed(free):
                vals[d] = lax.rem(rest, SIZE[d])
                rest = lax.div(rest, SIZE[d])
            full = []
            for d, fixed in zip(wdims, place(wdims, at)):
                full.append(vals[d] if d in vals else fixed)
            body(tuple(full), tuple(vals[d] for d in free))
            return 0

        if total == 1:
            one(jnp.int32(0), 0)
        else:
            lax.fori_loop(0, total, one, 0)

    f32 = jnp.float32

    def add(i, at, others, half=None, out=None):
        w = widths[i]
        lo, size = 0, w
        if half is not None:
            if "l" in wdims:
                at = {**at, "l": half}
            else:
                lo, size = half * (w // 2), w // 2

        def body(full, short):
            cut = (ALL, pl.ds(lo, size))
            total = work[i][full + cut].astype(f32)
            for ref, same in others:
                if same:
                    total = total + ref[full + cut].astype(f32)
                else:
                    total = total + ref[short + (ALL, ALL)].astype(f32)
            if out is None:
                work[i][full + cut] = total.astype(work[i].dtype)
            else:
                lead = (full[0],) if "l" in wdims else ()
                out[lead + (ALL, pl.ds(starts[i], w))] = total

        each_block(at, body)

    for phase in range(3):
        stage = {}

        def ctx_of(i):
            order = ORDERS[i]
            axis = order[phase]
            base = {"x": ALL, "y": ALL, "z": ALL}
            for done in order[:phase]:
                base[done] = me[done]
            return axis, base

        def at_of(i, by):
            axis, base = ctx_of(i)
            return {**base, axis: lax.rem(me[axis] + by + 4, 4)}

        def ready(i, step):
            if phase == 0:
                for c in loads[i, step]:
                    c.wait()
                for c in pairs[i, step]:
                    c.wait_recv()
                add(i, at_of(i, TURN[step]), [(sib[i], True)])

        for i in range(n):
            axis, _ = ctx_of(i)
            b = bufs[12 * i + 4 * phase : 12 * i + 4 * phase + 4]
            s, r = send.at[i, phase], recv.at[i, phase]
            ready(i, 0)
            right, left = device_at(moved(me, axis, 1)), device_at(moved(me, axis, -1))
            far = at_of(i, 2)
            one = remote(view(work[i], wdims, far, (0, widths[i]), 0), b[0], s.at[0], r.at[0], right)
            two = remote(view(work[i], wdims, far, (0, widths[i]), 1), b[1], s.at[1], r.at[1], left)
            stage[i] = [b, s, r, right, left, one, two]
        for i in range(n):
            b, s, r, right, left, one, two = stage[i]
            ready(i, 1)
            one.wait_recv()
            add(i, at_of(i, 1), [(b[0], False)], 0)
            three = remote(view(work[i], wdims, at_of(i, 1), (0, widths[i])), b[2], s.at[2], r.at[2], right)
            ready(i, 2)
            two.wait_recv()
            add(i, at_of(i, -1), [(b[1], False)], 1)
            four = remote(view(work[i], wdims, at_of(i, -1), (0, widths[i])), b[3], s.at[3], r.at[3], left)
            stage[i] = [b, three, four]
            pending += [one, two, three, four]
        for i in range(n):
            b, three, four = stage[i]
            ready(i, 3)
            three.wait_recv()
            four.wait_recv()
            add(i, at_of(i, 0), [(b[2], False), (b[3], False)], None, out_ref if phase == 2 else None)
    for c in pending:
        c.wait_send()
    for k in pairs:
        for c in pairs[k]:
            c.wait_send()
    for c in swaps:
        c.wait()


def scatter(ins, dims, parts, rows, name, collective_id, vmem, trades=()):
    n = len(parts)
    wdims = tuple(d for d in dims if d != "c")
    widths = [sum(width for _, (_, width), _, _ in sources) for sources in parts]
    wshape = tuple(SIZE[d] for d in wdims)
    dt = ins[0].dtype
    scratch = [pltpu.VMEM(wshape + (rows, w), dt) for w in widths] * 2
    for i in range(n):
        for phase in range(3):
            gone = set(ORDERS[i][: phase + 1])
            left = [d for d in wdims if ("z" if d in ("zh", "zl") else d) not in gone]
            shape = tuple(SIZE[d] for d in left)
            small = tuple(SIZE[d] for d in left if d != "l")
            halfw = widths[i] if "l" in dims else widths[i] // 2
            scratch += [pltpu.VMEM(small + (rows, halfw), dt)] * 2
            scratch += [pltpu.VMEM(shape + (rows, widths[i]), dt)] * 2
    most = max(len(s) for s in parts)
    scratch += [
        pltpu.SemaphoreType.DMA((n, 4, most)),
        pltpu.SemaphoreType.DMA((n, 4, most)),
        pltpu.SemaphoreType.DMA((n, 4, most)),
        pltpu.SemaphoreType.DMA((n, 3, 4)),
        pltpu.SemaphoreType.DMA((n, 3, 4)),
        pltpu.SemaphoreType.DMA((max(1, len(trades)), 3)),
    ]
    anywhere = pl.BlockSpec(memory_space=pl.ANY)
    lead = (2,) if "l" in dims else ()
    return pl.pallas_call(
        functools.partial(scatter_kernel, dims, parts, len(ins), len(trades)),
        out_shape=(
            jax.ShapeDtypeStruct(lead + (rows, sum(widths)), jnp.float32),
            *(jax.ShapeDtypeStruct(t.shape, t.dtype) for t in trades),
        ),
        in_specs=[anywhere] * (len(ins) + len(trades)),
        out_specs=(pl.BlockSpec(memory_space=pltpu.VMEM),) + (anywhere,) * len(trades),
        scratch_shapes=scratch,
        compiler_params=pltpu.CompilerParams(
            collective_id=collective_id, has_side_effects=True, vmem_limit_bytes=vmem
        ),
        name=name,
    )(*ins, *trades)


W_DIMS = ("zl", "zh", "x", "y", "c")
W_PARTS = ((0, 1792), (1792, 1792), (3584, 1792))
T_DIMS = ("l", "zh", "x", "y", "c", "zl")
T_PARTS = ((0, 256), (256, 256), (512, 128))


QH = 15
KEY_HEADS = 5
GROUPS = 3
HEAD_SIZE = 64
EPS = 1e-05
ROPE_BASE = 10000.0
NEGATIVE = -1e30
LOG2E = 1.4426950408889634
BLOCKS = 128
HALF = 64
SIDE = BLOCKS * HALF
LANES = GROUPS * HALF
CHUNK = 2048
BACK_CHUNK = 1024
UNROLL = 2
VMEM_LIMIT = 56 << 20


def chunk_ranges(side, own, size):
    count = SIDE // size
    if side == 0:
        diag = lax.div(HALF * own, size)
        first = HALF * (BLOCKS - own)
        edge, whole = lax.div(first, size), lax.div(first + size - 1, size)
        return ((diag, diag + 1), (0, diag)), ((edge, whole), (whole, count))
    rows = HALF * (own + 1)
    edge, whole = lax.div(rows, size), lax.div(rows + size - 1, size)
    diag = lax.div(HALF * (BLOCKS - 1 - own), size)
    return ((edge, whole), (0, edge)), ((diag, diag + 1), (diag + 1, count))


def seen(source, first, side, own, shape, keys):
    row = first + lax.broadcasted_iota(jnp.int32, shape, keys)
    block, place = row // HALF, row % HALF
    if source == 0:
        key = block * (2 * HALF) + place
    else:
        key = (BLOCKS - 1 - block) * (2 * HALF) + HALF + place
    col = lax.broadcasted_iota(jnp.int32, shape, 1 - keys)
    return key <= own * (2 * HALF) + side * HALF + col % HALF


def dot_nt(a, b):
    return lax.dot_general(a, b, (((1,), (1,)), ((), ())), preferred_element_type=jnp.float32)


def dot_tn(a, b):
    return lax.dot_general(a, b, (((0,), (0,)), ((), ())), preferred_element_type=jnp.float32)


def dot_nn(a, b):
    return lax.dot_general(a, b, (((1,), (0,)), ((), ())), preferred_element_type=jnp.float32)


def my_block():
    return lax.axis_index("ctx") * 2 + lax.axis_index("fsdp")


def attend_kernel(kv_ref, q_ref, o_ref, lse_ref, acc_ref):
    me = my_block()
    lanes = range(0, CHUNK, 128)
    for side in range(2):
        own = me if side == 0 else BLOCKS - 1 - me
        q = q_ref[0, side]
        acc_ref[...] = jnp.zeros_like(acc_ref)

        def step(source, masked, chunk, carry):
            peak, total = carry
            kv = kv_ref[source, pl.ds(pl.multiple_of(chunk * CHUNK, CHUNK), CHUNK), :]
            s = dot_nt(q, kv) * LOG2E
            if masked:
                s = jnp.where(seen(source, chunk * CHUNK, side, own, (LANES, CHUNK), 1), s, NEGATIVE)
            tops = functools.reduce(jnp.maximum, [s[:, k : k + 128] for k in lanes])
            new = jnp.maximum(peak, jnp.max(tops, 1, keepdims=True))
            p = jnp.exp2(s - new)
            scale = jnp.exp2(peak - new)
            total = total * scale + sum(p[:, k : k + 128] for k in lanes)
            acc_ref[...] = acc_ref[...] * scale + dot_nn(p.astype(jnp.bfloat16), kv)
            return new, total

        carry = (jnp.full((LANES, 1), NEGATIVE, jnp.float32), jnp.zeros((LANES, 128), jnp.float32))
        for source, (edge, whole) in enumerate(chunk_ranges(side, own, CHUNK)):
            carry = lax.fori_loop(edge[0], edge[1], functools.partial(step, source, True), carry)
            carry = lax.fori_loop(whole[0], whole[1], functools.partial(step, source, False), carry)
        peak, total = carry[0], jnp.sum(carry[1], 1, keepdims=True)
        o_ref[0, side] = (acc_ref[...] / total).T[HEAD_SIZE:, :]
        lse_ref[0, side] = jnp.broadcast_to(peak + jnp.log2(total), (LANES, 128)).T[:1, :]


def attend(kv, q):
    return pl.pallas_call(
        attend_kernel,
        grid=(KEY_HEADS,),
        out_shape=(
            jax.ShapeDtypeStruct((KEY_HEADS, 2, HEAD_SIZE, LANES), jnp.float32),
            jax.ShapeDtypeStruct((KEY_HEADS, 2, 1, LANES), jnp.float32),
        ),
        in_specs=[
            pl.BlockSpec((2, SIDE, 128), lambda h: (0, 0, h)),
            pl.BlockSpec((1, 2, LANES, 128), lambda h: (h, 0, 0, 0)),
        ],
        out_specs=(
            pl.BlockSpec((1, 2, HEAD_SIZE, LANES), lambda h: (h, 0, 0, 0)),
            pl.BlockSpec((1, 2, 1, LANES), lambda h: (h, 0, 0, 0)),
        ),
        scratch_shapes=[pltpu.VMEM((LANES, 128), jnp.float32)],
        compiler_params=pltpu.CompilerParams(vmem_limit_bytes=VMEM_LIMIT),
        name="attend",
    )(kv, q)


def attend_back_kernel(kv_ref, q_ref, do_ref, lse_ref, delta_ref, dq_ref, dkv_ref, acc_ref):
    me = my_block()
    dkv_ref[...] = jnp.zeros_like(dkv_ref)
    for side in range(2):
        own = me if side == 0 else BLOCKS - 1 - me
        q, do = q_ref[0, side], do_ref[0, side]
        lse, delta = lse_ref[0, side], delta_ref[0, side]
        acc_ref[...] = jnp.zeros_like(acc_ref)

        def step(source, masked, width, first, chunk, carry):
            dq = 0.0
            for u in range(width):
                at = first + (chunk - first) * width + u
                rows = pl.ds(pl.multiple_of(at * BACK_CHUNK, BACK_CHUNK), BACK_CHUNK)
                kv = kv_ref[source, rows, :]
                p = jnp.exp2(dot_nt(kv, q) * LOG2E - lse)
                if masked:
                    p = jnp.where(seen(source, at * BACK_CHUNK, side, own, (BACK_CHUNK, LANES), 0), p, 0.0)
                ds = (p * (dot_nt(kv, do) - delta)).astype(jnp.bfloat16)
                more = dot_nn(ds, q) + dot_nn(p.astype(jnp.bfloat16), do)
                dkv_ref[source, rows, :] = (dkv_ref[source, rows, :].astype(jnp.float32) + more).astype(jnp.bfloat16)
                dq = dq + dot_tn(kv, ds)
            acc_ref[...] += dq
            return carry

        for source, (edge, whole) in enumerate(chunk_ranges(side, own, BACK_CHUNK)):
            lax.fori_loop(edge[0], edge[1], functools.partial(step, source, True, 1, edge[0]), 0)
            start, end = whole
            for width in (UNROLL, 1):
                count = lax.div(end - start, width)
                lax.fori_loop(start, start + count, functools.partial(step, source, False, width, start), 0)
                start = start + count * width
        dq_ref[0, side] = acc_ref[:HEAD_SIZE, :]


def attend_back(kv, q, do, lse, delta):
    per_head = pl.BlockSpec((1, 2, LANES, 128), lambda h: (h, 0, 0, 0))
    row = pl.BlockSpec((1, 2, 1, LANES), lambda h: (h, 0, 0, 0))
    keys = pl.BlockSpec((2, SIDE, 128), lambda h: (0, 0, h))
    return pl.pallas_call(
        attend_back_kernel,
        grid=(KEY_HEADS,),
        out_shape=(
            jax.ShapeDtypeStruct((KEY_HEADS, 2, HEAD_SIZE, LANES), jnp.float32),
            jax.ShapeDtypeStruct(kv.shape, jnp.bfloat16),
        ),
        in_specs=[keys, per_head, per_head, row, row],
        out_specs=(pl.BlockSpec((1, 2, HEAD_SIZE, LANES), lambda h: (h, 0, 0, 0)), keys),
        scratch_shapes=[pltpu.VMEM((128, LANES), jnp.float32)],
        compiler_params=pltpu.CompilerParams(vmem_limit_bytes=VMEM_LIMIT),
        name="attend_back",
    )(kv, q, do, lse, delta)


def rotary_tables(positions):
    half = HEAD_SIZE // 2
    freq = ROPE_BASE ** (-(jnp.arange(half, dtype=jnp.float32) * 2.0 / HEAD_SIZE))
    angle = positions.astype(jnp.float32)[:, None] * freq[None, :]
    return (jnp.cos(angle)[:, None, :], jnp.sin(angle)[:, None, :])


def rotate(values, cosine, sine):
    count = values.shape[0]
    half = HEAD_SIZE // 2
    heads = values.reshape(count, -1, HEAD_SIZE)
    first = heads[..., :half]
    second = heads[..., half:]
    return jnp.concatenate(
        [first * cosine - second * sine, second * cosine + first * sine], -1
    ).reshape(count, -1)


def mm(form, left, right):
    return jnp.einsum(form, left, right, preferred_element_type=jnp.float32)


def by_head(rows):
    r = rows.reshape(2, HALF, KEY_HEADS, GROUPS, HEAD_SIZE)
    return jnp.transpose(r, (2, 0, 3, 1, 4)).reshape(KEY_HEADS, 2, LANES, HEAD_SIZE)


def by_token(heads):
    h = heads.reshape(KEY_HEADS, 2, HEAD_SIZE, GROUPS, HALF)
    return jnp.transpose(h, (1, 4, 0, 3, 2)).reshape(2 * HALF, QH * HEAD_SIZE)


def outer_kernel(left_ref, right_ref, out_ref):
    out_ref[0] = dot_tn(left_ref[...], right_ref[0]).astype(jnp.bfloat16)


def outer(left, right, steps):
    tokens, m = left.shape
    n = right.shape[-1]
    return pl.pallas_call(
        outer_kernel,
        grid=(2, steps),
        out_shape=jax.ShapeDtypeStruct((2, m, n), jnp.bfloat16),
        in_specs=[
            pl.BlockSpec((tokens, m // steps), lambda h, s: (0, s)),
            pl.BlockSpec((1, tokens, n), lambda h, s: (h, 0, 0)),
        ],
        out_specs=pl.BlockSpec((1, m // steps, n), lambda h, s: (h, s, 0)),
        compiler_params=pltpu.CompilerParams(vmem_limit_bytes=VMEM_LIMIT),
        name="outer",
    )(left, right)


def thirds(rows):
    high = rows.astype(jnp.bfloat16)
    rest = rows - high.astype(jnp.float32)
    middle = rest.astype(jnp.bfloat16)
    return high, middle, (rest - middle.astype(jnp.float32)).astype(jnp.bfloat16)


def ffn_kernel(
    whole_ref, attn_ref, x_ref, dy_ref, gain_ref, spread_ref, spread_down_ref,
    layer_out_ref, middle_grad_ref, attn_grad_ref, attn_wide_ref, normed_ref, gate_low_ref, up_low_ref,
    inner_ref, middle_low_ref, gain_grad_ref,
    w_out, w_gate, w_up, w_down, gate_s, up_s, sems,
):
    bf, f32 = jnp.bfloat16, jnp.float32

    def fetch(dst, start, width, sem):
        c = pltpu.make_async_copy(whole_ref.at[:, :, :, pl.ds(start, width)], dst, sem)
        c.start()
        return c

    get_out = fetch(w_out, 3584, 512, sems.at[0])
    get_gate = fetch(w_gate, 0, 1280, sems.at[1])
    get_up = fetch(w_up, 1792, 1280, sems.at[2])
    get_down = [
        fetch(w_down.at[:, :, pl.ds(16 * g, 16), :], 1280 + 1792 * g, 512, sems.at[3 + g]) for g in range(3)
    ]
    real = lax.broadcasted_iota(jnp.int32, (128, 512), 1) < 480

    attn_wide = 0.0
    for h in range(2):
        attn_wide = attn_wide + dot_nn(attn_ref[h].astype(bf), spread_ref[h])
    attn_wide = attn_wide.astype(bf)
    attn_wide_ref[...] = attn_wide
    get_out.wait()
    middle, squares = [], 0.0
    for h in range(2):
        part = dot_nn(attn_wide, w_out[h].reshape(1024, 512))
        part = x_ref[h].astype(f32) + jnp.where(real, part, 0.0)
        squares = squares + jnp.sum(part * part, -1, keepdims=True)
        middle.append(part)
    factor = lax.rsqrt(squares / 960 + EPS)
    normed = 0.0
    for h in range(2):
        normed = normed + dot_nn((middle[h] * factor * gain_ref[h]).astype(bf), spread_ref[h])
    normed = normed.astype(bf)
    normed_ref[...] = normed
    get_gate.wait()
    get_up.wait()
    for h in range(2):
        gate = dot_nn(normed, w_gate[h].reshape(1024, 1280))
        up = dot_nn(normed, w_up[h].reshape(1024, 1280))
        gate_s[h], up_s[h] = gate, up
        inner = (gate * jax.nn.sigmoid(gate) * up).astype(bf)
        for b in range(2):
            inner_ref[:, pl.ds(768 * (2 * h + b), 768)] = dot_nn(
                inner[:, 640 * b : 640 * b + 640], spread_down_ref[...]
            ).astype(bf)
    for c in get_down:
        c.wait()
    for h in range(2):
        low = dot_nn(inner_ref[...], w_down[h].reshape(3072, 512))
        layer_out_ref[h] = (middle[h] + low).astype(bf)
    normed_grad = 0.0
    for h in range(2):
        for b in range(2):
            blocks = pl.ds(16 * (2 * h + b), 16)
            wide_grad = 0.0
            for d in range(2):
                wide_grad = wide_grad + dot_nt(dy_ref[d], w_down[d, blocks].reshape(768, 512))
            inner_grad = 0.0
            for t in thirds(wide_grad):
                inner_grad = inner_grad + dot_nt(t, spread_down_ref[...])
            cols = pl.ds(640 * b, 640)
            gate, up = gate_s[h, :, cols], up_s[h, :, cols]
            sigma = jax.nn.sigmoid(gate)
            gate_low_ref[h, :, cols] = (inner_grad * up * sigma * (1.0 + gate * (1.0 - sigma))).astype(bf)
            up_low_ref[h, :, cols] = (inner_grad * (gate * sigma)).astype(bf)
        normed_grad = normed_grad + dot_nt(gate_low_ref[h], w_gate[h].reshape(1024, 1280))
        normed_grad = normed_grad + dot_nt(up_low_ref[h], w_up[h].reshape(1024, 1280))
    split = thirds(normed_grad)
    grads, mean = [], 0.0
    for h in range(2):
        g = 0.0
        for t in split:
            g = g + dot_nt(t, spread_ref[h])
        gain_grad_ref[h] = jnp.sum(g * middle[h] * factor, 0, keepdims=True)
        g = g * gain_ref[h]
        mean = mean + jnp.sum(g * middle[h], -1, keepdims=True)
        grads.append(g)
    wide_grad = 0.0
    for h in range(2):
        total = dy_ref[h].astype(f32) + factor * grads[h] - middle[h] * (factor * factor * factor * (mean / 960))
        middle_grad_ref[h] = total
        middle_low_ref[h] = total.astype(bf)
        wide_grad = wide_grad + dot_nt(total.astype(bf), w_out[h].reshape(1024, 512))
    wide_grad = wide_grad.astype(bf)
    for h in range(2):
        attn_grad_ref[h] = dot_nt(wide_grad, spread_ref[h]).astype(bf)


def ffn(whole, attn, x, dy, gain, spread, spread_down):
    bf, f32 = jnp.bfloat16, jnp.float32
    vmem = pl.BlockSpec(memory_space=pltpu.VMEM)
    shapes = [
        ((2, 128, 512), bf), ((2, 128, 512), f32), ((2, 128, 512), bf), ((128, 1024), bf), ((128, 1024), bf),
        ((2, 128, 1280), bf), ((2, 128, 1280), bf), ((128, 3072), bf), ((2, 128, 512), bf), ((2, 1, 512), f32),
    ]
    return pl.pallas_call(
        ffn_kernel,
        out_shape=tuple(jax.ShapeDtypeStruct(s, d) for s, d in shapes),
        in_specs=[pl.BlockSpec(memory_space=pl.ANY)] + [vmem] * 6,
        out_specs=(vmem,) * len(shapes),
        scratch_shapes=[
            pltpu.VMEM((2, 64, 16, 512), bf),
            pltpu.VMEM((2, 64, 16, 1280), bf),
            pltpu.VMEM((2, 64, 16, 1280), bf),
            pltpu.VMEM((2, 64, 48, 512), bf),
            pltpu.VMEM((2, 128, 1280), f32),
            pltpu.VMEM((2, 128, 1280), f32),
            pltpu.SemaphoreType.DMA((6,)),
        ],
        compiler_params=pltpu.CompilerParams(vmem_limit_bytes=VMEM_LIMIT),
        name="ffn",
    )(whole, attn, x, dy, gain, spread, spread_down)


def halves(rows):
    both = jnp.stack([rows[:, :480], rows[:, 480:]])
    return jnp.pad(both, ((0, 0), (0, 0), (0, 32)))


def joined(both):
    return jnp.concatenate([both[0, :, :480], both[1, :, :480]], 1)


def local(
    layer_in,
    attn_gain,
    query_weight,
    key_weight,
    value_weight,
    output_weight,
    ffn_gain,
    gate_weight,
    up_weight,
    down_weight,
    out_cotangent,
):
    bf, f32 = jnp.bfloat16, jnp.float32
    me = my_block()

    down = jnp.zeros((48, 512), bf)
    down = down.at[:40, :480].set(down_weight)
    down = down.at[40, :15].set(attn_gain).at[41, :15].set(ffn_gain)
    down = down.reshape(3, 16, 512)
    oqkv = jnp.concatenate([output_weight, query_weight, key_weight, value_weight], 1)
    mats = [jnp.pad(a, ((0, 1), (0, 0))) for a in (gate_weight, up_weight, oqkv)]
    piece = jnp.concatenate([a for i in range(3) for a in (mats[i], down[i])], 1)
    whole, x_low, dy = gather(piece, W_DIMS, W_PARTS, "gather_weights", 1, (layer_in, out_cotangent))
    whole = whole.reshape(2, 64, 16, 5376)
    w_qkv = whole.reshape(2, 1024, 5376)[:, :, 4064:4864]
    gain_one = whole[0, :, 8, 4864:4880].reshape(1024).astype(f32)
    gain_two = whole[0, :, 9, 4864:4879].reshape(1, 960).astype(f32)

    i = lax.broadcasted_iota(jnp.int32, (2, 512, 1024), 1)
    d = i + 480 * lax.broadcasted_iota(jnp.int32, (2, 512, 1024), 0)
    j = lax.broadcasted_iota(jnp.int32, (2, 512, 1024), 2)
    spread = jnp.logical_and(i < 480, j == (d // 15) * 16 + d % 15).astype(bf)
    i = lax.broadcasted_iota(jnp.int32, (640, 768), 0)
    j = lax.broadcasted_iota(jnp.int32, (640, 768), 1)
    spread_down = (j == (i // 40) * 48 + i % 40).astype(bf)

    t = jnp.arange(HALF, dtype=jnp.int32)
    positions = jnp.concatenate([me * 128 + t, (BLOCKS - 1 - me) * 128 + HALF + t])
    cosine, sine = rotary_tables(positions)

    x_halves, dy_halves = halves(x_low), halves(dy)
    hidden = mm("htd,hde->te", x_halves, spread)
    factor_one = lax.rsqrt(jnp.sum(hidden * hidden, -1, keepdims=True) / 960 + EPS)
    normed = (hidden * factor_one * gain_one).astype(bf)
    qkv = mm("te,hec->thc", normed, w_qkv)
    query = qkv[:, :, :480].reshape(128, 960)
    key = qkv[:, :, 480:640].reshape(128, 320)
    value = qkv[:, :, 640:800].reshape(128, 320)
    query_rot = rotate(query, cosine, sine).astype(bf)
    key_rot = rotate(key, cosine, sine).astype(bf)
    kv_piece = jnp.concatenate(
        [key_rot.reshape(2, HALF, KEY_HEADS, 64), value.astype(bf).reshape(2, HALF, KEY_HEADS, 64)], -1
    ).reshape(2, HALF, 640)
    (kv,) = gather(kv_piece, T_DIMS, T_PARTS, "gather_keys", 2)
    kv = kv.reshape(2, SIDE, 640)
    q_heads = jnp.pad(by_head(query_rot * jnp.asarray(0.125, bf)), ((0, 0), (0, 0), (0, 0), (0, 64)))
    attn_heads, lse = attend(kv, q_heads)
    attn = by_token(attn_heads)
    (layer_out, middle_grad, attn_grad, attn_wide, normed_two, gate_low, up_low, inner, middle_low, gain_two_term) = ffn(
        whole, halves(attn), x_halves, dy_halves, halves(gain_two), spread, spread_down
    )
    layer_out, middle_grad, attn_grad = joined(layer_out), joined(middle_grad), joined(attn_grad)
    delta = jnp.sum((attn_grad.astype(f32) * attn).reshape(2, HALF, KEY_HEADS, GROUPS, HEAD_SIZE), -1)
    delta = jnp.transpose(delta, (2, 0, 3, 1)).reshape(KEY_HEADS, 2, 1, LANES)
    do_heads = jnp.pad(by_head(attn_grad), ((0, 0), (0, 0), (0, 0), (64, 0)))
    dq_heads, dkv = attend_back(kv, q_heads, do_heads, lse, delta)
    dkv = dkv.reshape(2, 2, 4, 4, 2, 2, HALF, 640)
    parts = tuple(((0, c, 0, ALL),) for c in T_PARTS)
    key_sums, layer_out = scatter([dkv], T_DIMS, parts, HALF, "scatter_keys", 3, VMEM_LIMIT, (layer_out,))
    key_sums = key_sums.reshape(128, KEY_HEADS, 128)
    query_low = rotate(by_token(dq_heads) * 0.125, cosine, -sine).astype(bf)
    key_low = rotate(key_sums[..., :64].reshape(128, 320), cosine, -sine).astype(bf)
    value_low = key_sums[..., 64:].reshape(128, 320).astype(bf)
    qkv_low = jnp.concatenate(
        [query_low.reshape(128, 2, 480), key_low.reshape(128, 2, 160), value_low.reshape(128, 2, 160)], -1
    )
    normed_grad = mm("thc,hec->te", qkv_low, w_qkv)
    weighted = gain_one * normed_grad
    input_back = factor_one * weighted - hidden * factor_one**3 * (
        jnp.sum(weighted * hidden, -1, keepdims=True) / 960
    )
    gain_one_term = jnp.sum(normed_grad * hidden * factor_one, 0)
    input_back = sum(mm("te,hde->htd", part, spread) for part in thirds(input_back))
    input_grad = middle_grad + joined(input_back)

    gains = jnp.concatenate([gain_one_term.reshape(64, 16)[:, :15], joined(gain_two_term).reshape(64, 15)], 1)
    gains = jnp.pad(gains.astype(bf), ((0, 0), (0, 1280 - 30)))
    right = jnp.concatenate(
        [
            jnp.pad(jnp.transpose(qkv_low, (1, 0, 2)), ((0, 0), (0, 0), (480, 0))),
            jnp.pad(middle_low[:, :, :480], ((0, 0), (0, 0), (0, 800))),
            jnp.stack([gains, gains]),
        ],
        1,
    )
    slot = lax.broadcasted_iota(jnp.int32, (64, 1024), 0) * 16 + 15
    slot = (slot == lax.broadcasted_iota(jnp.int32, (64, 1024), 1)).astype(bf)
    left = jnp.concatenate([normed, attn_wide, slot], 0)
    terms = [outer(normed_two, gate_low, 1), outer(normed_two, up_low, 1), outer(left, right, 1)]
    terms = [a.reshape(2, 2, 4, 4, 2, 16, 1280) for a in terms]
    terms.append(outer(inner, dy_halves, 1).reshape(2, 2, 4, 4, 2, 48, 512))
    parts = tuple(((k, (0, 1280), 0, ALL), (3, (0, 512), 1280, pl.ds(16 * k, 16))) for k in range(3))
    sums, input_grad = scatter(terms, W_DIMS, parts, 16, "scatter_weights", 4, VMEM_LIMIT, (input_grad,))
    down_sum = jnp.concatenate([sums[:, 1280:1792], sums[:, 3072:3584], sums[:, 4864:5376]], 0)
    return (
        layer_out,
        input_grad,
        sums[15, 3584:3599],
        sums[:15, 4064:4544],
        sums[:15, 4544:4704],
        sums[:15, 4704:4864],
        sums[:15, 3584:4064],
        sums[15, 3599:3614],
        sums[:15, :1280],
        sums[:15, 1792:3072],
        down_sum[:40, :480],
    )


def solution(mesh):
    matrix, tokens = P("ctx", "fsdp"), P(("ctx", "fsdp"), None)
    return jax.shard_map(
        local,
        mesh=mesh,
        in_specs=(tokens, P("ctx"), matrix, matrix, matrix, matrix, P("ctx"), matrix, matrix, matrix, tokens),
        out_specs=(tokens, tokens, P("ctx"), matrix, matrix, matrix, matrix, P("ctx"), matrix, matrix, matrix),
        check_vma=False,
    )
```

```python
import functools

import jax
import jax.numpy as jnp
from jax import lax
from jax.experimental import pallas as pl
from jax.experimental.pallas import tpu as pltpu
from jax.sharding import PartitionSpec as P

MESH = pl.DeviceIdType.MESH
ORDERS = (("x", "y", "z"), ("y", "z", "x"), ("z", "x", "y"))
ALL = slice(None)


def whereabouts():
    ctx = lax.axis_index("ctx")
    low = lax.axis_index("fsdp")
    return {
        "x": lax.rem(lax.div(ctx, 8), 4),
        "y": lax.rem(lax.div(ctx, 2), 4),
        "z": lax.div(ctx, 32) * 2 + low,
        "c": lax.rem(ctx, 2),
    }


def device_at(at):
    ctx = ((lax.div(at["z"], 2) * 4 + at["x"]) * 4 + at["y"]) * 2 + at["c"]
    return (ctx, lax.rem(at["z"], 2))


def moved(at, axis, by):
    size = 2 if axis == "c" else 4
    return {**at, axis: lax.rem(at[axis] + by + size, size)}


def mirror():
    return (63 - lax.axis_index("ctx"), 1 - lax.axis_index("fsdp"))


def greet(me):
    barrier = pltpu.get_barrier_semaphore()
    others = [moved(me, a, s) for a in "xyz" for s in (1, -1)] + [moved(me, "c", 1)]
    targets = [device_at(other) for other in others] + [mirror()]
    for target in targets:
        pl.semaphore_signal(barrier, inc=1, device_id=target, device_id_type=MESH)
    pl.semaphore_wait(barrier, len(targets))


def start_trades(pairs, sems):
    out = []
    for k, (src, dst) in enumerate(pairs):
        half = src.shape[0] // 2
        stay = pltpu.make_async_copy(src.at[pl.ds(0, half)], dst.at[pl.ds(0, half)], sems.at[k, 0])
        go = pltpu.make_async_remote_copy(
            src_ref=src.at[pl.ds(half, half)],
            dst_ref=dst.at[pl.ds(half, half)],
            send_sem=sems.at[k, 1],
            recv_sem=sems.at[k, 2],
            device_id=mirror(),
            device_id_type=MESH,
        )
        stay.start()
        go.start()
        out += [stay, go]
    return out


def place(dims, at):
    index = []
    for d in dims:
        if d in ("zh", "zl"):
            z = at["z"]
            index.append(ALL if z is ALL else (lax.div(z, 2) if d == "zh" else lax.rem(z, 2)))
        elif d == "l":
            index.append(at.get("l", ALL))
        else:
            index.append(at[d])
    return index


def view(ref, dims, at, cols, half=None, rows=ALL):
    start, width = cols
    if half is not None:
        if "l" in dims:
            at = {**at, "l": half}
        else:
            start, width = start + half * (width // 2), width // 2
    return ref.at[tuple(place(dims, at)) + (rows, pl.ds(start, width))]


def gather_kernel(dims, parts, trades, *refs):
    piece_ref, out_ref = refs[0], refs[1 + trades]
    send, recv, sib_send, sib_recv, own_sem, trade_sem = refs[2 + 2 * trades :]
    me = whereabouts()
    greet(me)
    swaps = start_trades(list(zip(refs[1 : 1 + trades], refs[2 + trades : 2 + 2 * trades])), trade_sem)
    sibling = device_at(moved(me, "c", 1))

    def copy(src, dst, ssem, rsem, to):
        c = pltpu.make_async_remote_copy(
            src_ref=src, dst_ref=dst, send_sem=ssem, recv_sem=rsem, device_id=to, device_id_type=MESH
        )
        c.start()
        return c

    pending = []
    mine = out_ref.at[tuple(place(dims, me)) + (ALL, ALL)]
    own = pltpu.make_async_copy(piece_ref, mine, own_sem)
    own.start()
    own.wait()
    for phase in range(3):
        stage = {}
        for i, cols in enumerate(parts):
            order = ORDERS[i]
            axis = order[phase]
            base = dict(me)
            for done in order[:phase]:
                base[done] = ALL
            right, left = moved(me, axis, 1), moved(me, axis, -1)

            def blk(by, half=None, base=base, axis=axis, cols=cols):
                at = {**base, axis: lax.rem(me[axis] + by + 4, 4)}
                return view(out_ref, dims, at, cols, half)

            s, r = send.at[i, phase], recv.at[i, phase]
            to_right = copy(blk(0), blk(0), s.at[0], r.at[0], device_at(right))
            to_left = copy(blk(0), blk(0), s.at[1], r.at[1], device_at(left))
            sibs = []
            if phase == 2:
                sibs.append(copy(blk(0), blk(0), sib_send.at[i, 0], sib_recv.at[i, 0], sibling))
            stage[i] = (blk, s, r, to_right, to_left, sibs, right, left)
        for i in range(len(parts)):
            blk, s, r, to_right, to_left, sibs, right, left = stage[i]
            to_right.wait_recv()
            on_right = copy(blk(-1, 0), blk(-1, 0), s.at[2], r.at[2], device_at(right))
            if phase == 2:
                sibs.append(copy(blk(-1), blk(-1), sib_send.at[i, 1], sib_recv.at[i, 1], sibling))
            to_left.wait_recv()
            on_left = copy(blk(1, 1), blk(1, 1), s.at[3], r.at[3], device_at(left))
            if phase == 2:
                sibs.append(copy(blk(1), blk(1), sib_send.at[i, 2], sib_recv.at[i, 2], sibling))
            pending += [to_right, to_left, on_right, on_left]
            stage[i] = (blk, sibs, on_right, on_left)
        for i in range(len(parts)):
            blk, sibs, on_right, on_left = stage[i]
            on_right.wait_recv()
            on_left.wait_recv()
            if phase == 2:
                sibs.append(copy(blk(2), blk(2), sib_send.at[i, 3], sib_recv.at[i, 3], sibling))
                pending += sibs
        if phase == 2:
            for i in range(len(parts)):
                for c in stage[i][1]:
                    c.wait_recv()
    for c in pending:
        c.wait_send()
    for c in swaps:
        c.wait()


SIZE = {"zl": 2, "zh": 2, "x": 4, "y": 4, "c": 2, "l": 2}


def gather(piece, dims, parts, name, collective_id, trades=()):
    shape = tuple(SIZE[d] for d in dims) + piece.shape[-2:]
    n = len(parts)
    anywhere = pl.BlockSpec(memory_space=pl.ANY)
    return pl.pallas_call(
        functools.partial(gather_kernel, dims, parts, len(trades)),
        out_shape=(
            jax.ShapeDtypeStruct(shape, piece.dtype),
            *(jax.ShapeDtypeStruct(t.shape, t.dtype) for t in trades),
        ),
        in_specs=[anywhere] * (1 + len(trades)),
        out_specs=(anywhere,) * (1 + len(trades)),
        scratch_shapes=[
            pltpu.SemaphoreType.DMA((n, 3, 4)),
            pltpu.SemaphoreType.DMA((n, 3, 4)),
            pltpu.SemaphoreType.DMA((n, 4)),
            pltpu.SemaphoreType.DMA((n, 4)),
            pltpu.SemaphoreType.DMA,
            pltpu.SemaphoreType.DMA((max(1, len(trades)), 3)),
        ],
        compiler_params=pltpu.CompilerParams(collective_id=collective_id, has_side_effects=True),
        name=name,
    )(piece, *trades)


def scatter_kernel(dims, parts, n_in, trades, *refs):
    ins, refs = refs[:n_in], refs[n_in:]
    kept, out_ref, given, refs = refs[:trades], refs[trades], refs[trades + 1 : 2 * trades + 1], refs[2 * trades + 1 :]
    n = len(parts)
    work, sib = refs[:n], refs[n : 2 * n]
    bufs = refs[2 * n : 2 * n + 12 * n]
    load_sem, sib_send, sib_recv, send, recv, trade_sem = refs[14 * n :]
    wdims = tuple(d for d in dims if d != "c")
    me = whereabouts()
    other = moved(me, "c", 1)
    sibling = device_at(other)
    widths = [w.shape[-1] for w in work]
    starts = [sum(widths[:i]) for i in range(n)]

    def remote(src, dst, ssem, rsem, to):
        c = pltpu.make_async_remote_copy(
            src_ref=src, dst_ref=dst, send_sem=ssem, recv_sem=rsem, device_id=to, device_id_type=MESH
        )
        c.start()
        return c

    loads, pairs = {}, {}
    TURN = (2, 1, -1, 0)

    def own_loads(step):
        for i, sources in enumerate(parts):
            axis = ORDERS[i][0]
            at = {"x": ALL, "y": ALL, "z": ALL, "c": me["c"], axis: lax.rem(me[axis] + TURN[step] + 4, 4)}
            loads[i, step] = []
            for j, (k, (c0, width), d0, rows) in enumerate(sources):
                c = pltpu.make_async_copy(
                    view(ins[k], dims, at, (c0, width), None, rows),
                    view(work[i], wdims, at, (d0, width)),
                    load_sem.at[i, step, j],
                )
                c.start()
                loads[i, step].append(c)

    def sib_sends(step):
        for i, sources in enumerate(parts):
            axis = ORDERS[i][0]
            at = {"x": ALL, "y": ALL, "z": ALL, "c": other["c"], axis: lax.rem(me[axis] + TURN[step] + 4, 4)}
            pairs[i, step] = []
            for j, (k, (c0, width), d0, rows) in enumerate(sources):
                pairs[i, step].append(
                    remote(
                        view(ins[k], dims, at, (c0, width), None, rows),
                        view(sib[i], wdims, at, (d0, width)),
                        sib_send.at[i, step, j],
                        sib_recv.at[i, step, j],
                        sibling,
                    )
                )

    own_loads(0)
    greet(me)
    for step in range(4):
        sib_sends(step)
        if step:
            own_loads(step)
    swaps = start_trades(list(zip(kept, given)), trade_sem)
    pending = []

    def each_block(at, body):
        free = [d for d in wdims if (at["z"] if d in ("zh", "zl") else at.get(d, ALL)) is ALL]
        total = 1
        for d in free:
            total *= SIZE[d]

        def one(t, _):
            vals, rest = {}, t
            for d in reversed(free):
                vals[d] = lax.rem(rest, SIZE[d])
                rest = lax.div(rest, SIZE[d])
            full = []
            for d, fixed in zip(wdims, place(wdims, at)):
                full.append(vals[d] if d in vals else fixed)
            body(tuple(full), tuple(vals[d] for d in free))
            return 0

        if total == 1:
            one(jnp.int32(0), 0)
        else:
            lax.fori_loop(0, total, one, 0)

    f32 = jnp.float32

    def add(i, at, others, half=None, out=None):
        w = widths[i]
        lo, size = 0, w
        if half is not None:
            if "l" in wdims:
                at = {**at, "l": half}
            else:
                lo, size = half * (w // 2), w // 2

        def body(full, short):
            cut = (ALL, pl.ds(lo, size))
            total = work[i][full + cut].astype(f32)
            for ref, same in others:
                if same:
                    total = total + ref[full + cut].astype(f32)
                else:
                    total = total + ref[short + (ALL, ALL)].astype(f32)
            if out is None:
                work[i][full + cut] = total.astype(work[i].dtype)
            else:
                lead = (full[0],) if "l" in wdims else ()
                out[lead + (ALL, pl.ds(starts[i], w))] = total

        each_block(at, body)

    for phase in range(3):
        stage = {}

        def ctx_of(i):
            order = ORDERS[i]
            axis = order[phase]
            base = {"x": ALL, "y": ALL, "z": ALL}
            for done in order[:phase]:
                base[done] = me[done]
            return axis, base

        def at_of(i, by):
            axis, base = ctx_of(i)
            return {**base, axis: lax.rem(me[axis] + by + 4, 4)}

        def ready(i, step):
            if phase == 0:
                for c in loads[i, step]:
                    c.wait()
                for c in pairs[i, step]:
                    c.wait_recv()
                add(i, at_of(i, TURN[step]), [(sib[i], True)])

        for i in range(n):
            axis, _ = ctx_of(i)
            b = bufs[12 * i + 4 * phase : 12 * i + 4 * phase + 4]
            s, r = send.at[i, phase], recv.at[i, phase]
            ready(i, 0)
            right, left = device_at(moved(me, axis, 1)), device_at(moved(me, axis, -1))
            far = at_of(i, 2)
            one = remote(view(work[i], wdims, far, (0, widths[i]), 0), b[0], s.at[0], r.at[0], right)
            two = remote(view(work[i], wdims, far, (0, widths[i]), 1), b[1], s.at[1], r.at[1], left)
            stage[i] = [b, s, r, right, left, one, two]
        for i in range(n):
            b, s, r, right, left, one, two = stage[i]
            ready(i, 1)
            one.wait_recv()
            add(i, at_of(i, 1), [(b[0], False)], 0)
            three = remote(view(work[i], wdims, at_of(i, 1), (0, widths[i])), b[2], s.at[2], r.at[2], right)
            ready(i, 2)
            two.wait_recv()
            add(i, at_of(i, -1), [(b[1], False)], 1)
            four = remote(view(work[i], wdims, at_of(i, -1), (0, widths[i])), b[3], s.at[3], r.at[3], left)
            stage[i] = [b, three, four]
            pending += [one, two, three, four]
        for i in range(n):
            b, three, four = stage[i]
            ready(i, 3)
            three.wait_recv()
            four.wait_recv()
            add(i, at_of(i, 0), [(b[2], False), (b[3], False)], None, out_ref if phase == 2 else None)
    for c in pending:
        c.wait_send()
    for k in pairs:
        for c in pairs[k]:
            c.wait_send()
    for c in swaps:
        c.wait()


def scatter(ins, dims, parts, rows, name, collective_id, vmem, trades=()):
    n = len(parts)
    wdims = tuple(d for d in dims if d != "c")
    widths = [sum(width for _, (_, width), _, _ in sources) for sources in parts]
    wshape = tuple(SIZE[d] for d in wdims)
    dt = ins[0].dtype
    scratch = [pltpu.VMEM(wshape + (rows, w), dt) for w in widths] * 2
    for i in range(n):
        for phase in range(3):
            gone = set(ORDERS[i][: phase + 1])
            left = [d for d in wdims if ("z" if d in ("zh", "zl") else d) not in gone]
            shape = tuple(SIZE[d] for d in left)
            small = tuple(SIZE[d] for d in left if d != "l")
            halfw = widths[i] if "l" in dims else widths[i] // 2
            scratch += [pltpu.VMEM(small + (rows, halfw), dt)] * 2
            scratch += [pltpu.VMEM(shape + (rows, widths[i]), dt)] * 2
    most = max(len(s) for s in parts)
    scratch += [
        pltpu.SemaphoreType.DMA((n, 4, most)),
        pltpu.SemaphoreType.DMA((n, 4, most)),
        pltpu.SemaphoreType.DMA((n, 4, most)),
        pltpu.SemaphoreType.DMA((n, 3, 4)),
        pltpu.SemaphoreType.DMA((n, 3, 4)),
        pltpu.SemaphoreType.DMA((max(1, len(trades)), 3)),
    ]
    anywhere = pl.BlockSpec(memory_space=pl.ANY)
    lead = (2,) if "l" in dims else ()
    return pl.pallas_call(
        functools.partial(scatter_kernel, dims, parts, len(ins), len(trades)),
        out_shape=(
            jax.ShapeDtypeStruct(lead + (rows, sum(widths)), jnp.float32),
            *(jax.ShapeDtypeStruct(t.shape, t.dtype) for t in trades),
        ),
        in_specs=[anywhere] * (len(ins) + len(trades)),
        out_specs=(pl.BlockSpec(memory_space=pltpu.VMEM),) + (anywhere,) * len(trades),
        scratch_shapes=scratch,
        compiler_params=pltpu.CompilerParams(
            collective_id=collective_id, has_side_effects=True, vmem_limit_bytes=vmem
        ),
        name=name,
    )(*ins, *trades)


W_DIMS = ("zl", "zh", "x", "y", "c")
FIRST_PARTS = ((0, 512), (512, 512), (1024, 256))
REST_PARTS = ((0, 1280), (1280, 1280), (2560, 1536))
T_DIMS = ("l", "zh", "x", "y", "c", "zl")
T_PARTS = ((0, 256), (256, 256), (512, 128))


QH = 15
KEY_HEADS = 5
GROUPS = 3
HEAD_SIZE = 64
EPS = 1e-05
ROPE_BASE = 10000.0
NEGATIVE = -1e30
LOG2E = 1.4426950408889634
BLOCKS = 128
HALF = 64
SIDE = BLOCKS * HALF
LANES = GROUPS * HALF
CHUNK = 2048
BACK_CHUNK = 1024
UNROLL = 2
VMEM_LIMIT = 56 << 20


def chunk_ranges(side, own, size):
    count = SIDE // size
    if side == 0:
        diag = lax.div(HALF * own, size)
        first = HALF * (BLOCKS - own)
        edge, whole = lax.div(first, size), lax.div(first + size - 1, size)
        return ((diag, diag + 1), (0, diag)), ((edge, whole), (whole, count))
    rows = HALF * (own + 1)
    edge, whole = lax.div(rows, size), lax.div(rows + size - 1, size)
    diag = lax.div(HALF * (BLOCKS - 1 - own), size)
    return ((edge, whole), (0, edge)), ((diag, diag + 1), (diag + 1, count))


def seen(source, first, side, own, shape, keys):
    row = first + lax.broadcasted_iota(jnp.int32, shape, keys)
    block, place = row // HALF, row % HALF
    if source == 0:
        key = block * (2 * HALF) + place
    else:
        key = (BLOCKS - 1 - block) * (2 * HALF) + HALF + place
    col = lax.broadcasted_iota(jnp.int32, shape, 1 - keys)
    return key <= own * (2 * HALF) + side * HALF + col % HALF


def dot_nt(a, b):
    return lax.dot_general(a, b, (((1,), (1,)), ((), ())), preferred_element_type=jnp.float32)


def dot_tn(a, b):
    return lax.dot_general(a, b, (((0,), (0,)), ((), ())), preferred_element_type=jnp.float32)


def dot_nn(a, b):
    return lax.dot_general(a, b, (((1,), (0,)), ((), ())), preferred_element_type=jnp.float32)


def my_block():
    return lax.axis_index("ctx") * 2 + lax.axis_index("fsdp")


def gather_steps(dims, parts, piece_ref, out_ref, sems):
    send, recv, sib_send, sib_recv, own_sem = sems
    me = whereabouts()
    sibling = device_at(moved(me, "c", 1))
    rings, sibs = {}, {}
    for i, cols in enumerate(parts):
        for phase in range(3):
            axis = ORDERS[i][phase]
            base = dict(me)
            for done in ORDERS[i][:phase]:
                base[done] = ALL

            def blk(by, half=None, base=base, axis=axis, cols=cols):
                at = {**base, axis: lax.rem(me[axis] + by + 4, 4)}
                return view(out_ref, dims, at, cols, half)

            right, left = device_at(moved(me, axis, 1)), device_at(moved(me, axis, -1))
            moves = ((blk(0), right), (blk(0), left), (blk(-1, 0), right), (blk(1, 1), left))
            rings[i, phase] = [
                pltpu.make_async_remote_copy(
                    src_ref=ref,
                    dst_ref=ref,
                    send_sem=send.at[i, phase, k],
                    recv_sem=recv.at[i, phase, k],
                    device_id=to,
                    device_id_type=MESH,
                )
                for k, (ref, to) in enumerate(moves)
            ]
            if phase == 2:
                sibs[i] = [
                    pltpu.make_async_remote_copy(
                        src_ref=blk(by),
                        dst_ref=blk(by),
                        send_sem=sib_send.at[i, k],
                        recv_sem=sib_recv.at[i, k],
                        device_id=sibling,
                        device_id_type=MESH,
                    )
                    for k, by in enumerate((0, -1, 1, 2))
                ]
    own = pltpu.make_async_copy(piece_ref, out_ref.at[tuple(place(dims, me)) + (ALL, ALL)], own_sem)
    count = range(len(parts))

    def step(k):
        phase = k // 2
        if k == 0:
            greet(me)
            own.start()
            own.wait()
        if k % 2 == 0:
            for i in count:
                if 0 < phase:
                    rings[i, phase - 1][2].wait_recv()
                    rings[i, phase - 1][3].wait_recv()
                if phase < 3:
                    rings[i, phase][0].start()
                    rings[i, phase][1].start()
                if phase == 2:
                    sibs[i][0].start()
                if phase == 3:
                    sibs[i][3].start()
        elif phase < 3:
            for i in count:
                for side in range(2):
                    rings[i, phase][side].wait_recv()
                    rings[i, phase][2 + side].start()
                    if phase == 2:
                        sibs[i][1 + side].start()
        else:
            for i in count:
                for c in sibs[i]:
                    c.wait_recv()
                    c.wait_send()
                for phase in range(3):
                    for c in rings[i, phase]:
                        c.wait_send()

    return step


def attend_kernel(kv_ref, q_ref, piece_ref, o_ref, lse_ref, rest_ref, acc_ref, *sems):
    me = my_block()
    head = pl.program_id(0)
    transfer = gather_steps(W_DIMS, REST_PARTS, piece_ref, rest_ref, sems)
    lanes = range(0, CHUNK, 128)
    for side in range(2):
        for turn in range(KEY_HEADS - 1):
            if 2 * turn + side < 7:
                pl.when(head == turn)(functools.partial(transfer, 2 * turn + side))
        own = me if side == 0 else BLOCKS - 1 - me
        q = q_ref[0, side]
        acc_ref[...] = jnp.zeros_like(acc_ref)

        def step(source, masked, chunk, carry):
            peak, total = carry
            kv = kv_ref[source, pl.ds(pl.multiple_of(chunk * CHUNK, CHUNK), CHUNK), :]
            s = dot_nt(q, kv) * LOG2E
            if masked:
                s = jnp.where(seen(source, chunk * CHUNK, side, own, (LANES, CHUNK), 1), s, NEGATIVE)
            tops = functools.reduce(jnp.maximum, [s[:, k : k + 128] for k in lanes])
            new = jnp.maximum(peak, jnp.max(tops, 1, keepdims=True))
            p = jnp.exp2(s - new)
            scale = jnp.exp2(peak - new)
            total = total * scale + sum(p[:, k : k + 128] for k in lanes)
            acc_ref[...] = acc_ref[...] * scale + dot_nn(p.astype(jnp.bfloat16), kv)
            return new, total

        carry = (jnp.full((LANES, 1), NEGATIVE, jnp.float32), jnp.zeros((LANES, 128), jnp.float32))
        for source, (edge, whole) in enumerate(chunk_ranges(side, own, CHUNK)):
            carry = lax.fori_loop(edge[0], edge[1], functools.partial(step, source, True), carry)
            carry = lax.fori_loop(whole[0], whole[1], functools.partial(step, source, False), carry)
        peak, total = carry[0], jnp.sum(carry[1], 1, keepdims=True)
        o_ref[0, side] = (acc_ref[...] / total).T[HEAD_SIZE:, :]
        lse_ref[0, side] = jnp.broadcast_to(peak + jnp.log2(total), (LANES, 128)).T[:1, :]
    pl.when(head == KEY_HEADS - 1)(functools.partial(transfer, 7))


def attend(kv, q, piece):
    n = len(REST_PARTS)
    return pl.pallas_call(
        attend_kernel,
        grid=(KEY_HEADS,),
        out_shape=(
            jax.ShapeDtypeStruct((KEY_HEADS, 2, HEAD_SIZE, LANES), jnp.float32),
            jax.ShapeDtypeStruct((KEY_HEADS, 2, 1, LANES), jnp.float32),
            jax.ShapeDtypeStruct((2, 2, 4, 4, 2) + piece.shape, piece.dtype),
        ),
        in_specs=[
            pl.BlockSpec((2, SIDE, 128), lambda h: (0, 0, h)),
            pl.BlockSpec((1, 2, LANES, 128), lambda h: (h, 0, 0, 0)),
            pl.BlockSpec(memory_space=pl.ANY),
        ],
        out_specs=(
            pl.BlockSpec((1, 2, HEAD_SIZE, LANES), lambda h: (h, 0, 0, 0)),
            pl.BlockSpec((1, 2, 1, LANES), lambda h: (h, 0, 0, 0)),
            pl.BlockSpec(memory_space=pl.ANY),
        ),
        scratch_shapes=[
            pltpu.VMEM((LANES, 128), jnp.float32),
            pltpu.SemaphoreType.DMA((n, 3, 4)),
            pltpu.SemaphoreType.DMA((n, 3, 4)),
            pltpu.SemaphoreType.DMA((n, 4)),
            pltpu.SemaphoreType.DMA((n, 4)),
            pltpu.SemaphoreType.DMA,
        ],
        compiler_params=pltpu.CompilerParams(
            collective_id=5, has_side_effects=True, vmem_limit_bytes=VMEM_LIMIT
        ),
        name="attend",
    )(kv, q, piece)


def attend_back_kernel(kv_ref, q_ref, do_ref, lse_ref, delta_ref, dq_ref, dkv_ref, acc_ref):
    me = my_block()
    dkv_ref[...] = jnp.zeros_like(dkv_ref)
    for side in range(2):
        own = me if side == 0 else BLOCKS - 1 - me
        q, do = q_ref[0, side], do_ref[0, side]
        lse, delta = lse_ref[0, side], delta_ref[0, side]
        acc_ref[...] = jnp.zeros_like(acc_ref)

        def step(source, masked, width, first, chunk, carry):
            dq = 0.0
            for u in range(width):
                at = first + (chunk - first) * width + u
                rows = pl.ds(pl.multiple_of(at * BACK_CHUNK, BACK_CHUNK), BACK_CHUNK)
                kv = kv_ref[source, rows, :]
                p = jnp.exp2(dot_nt(kv, q) * LOG2E - lse)
                if masked:
                    p = jnp.where(seen(source, at * BACK_CHUNK, side, own, (BACK_CHUNK, LANES), 0), p, 0.0)
                ds = (p * (dot_nt(kv, do) - delta)).astype(jnp.bfloat16)
                more = dot_nn(ds, q) + dot_nn(p.astype(jnp.bfloat16), do)
                dkv_ref[source, rows, :] = (dkv_ref[source, rows, :].astype(jnp.float32) + more).astype(jnp.bfloat16)
                dq = dq + dot_tn(kv, ds)
            acc_ref[...] += dq
            return carry

        for source, (edge, whole) in enumerate(chunk_ranges(side, own, BACK_CHUNK)):
            lax.fori_loop(edge[0], edge[1], functools.partial(step, source, True, 1, edge[0]), 0)
            start, end = whole
            for width in (UNROLL, 1):
                count = lax.div(end - start, width)
                lax.fori_loop(start, start + count, functools.partial(step, source, False, width, start), 0)
                start = start + count * width
        dq_ref[0, side] = acc_ref[:HEAD_SIZE, :]


def attend_back(kv, q, do, lse, delta):
    per_head = pl.BlockSpec((1, 2, LANES, 128), lambda h: (h, 0, 0, 0))
    row = pl.BlockSpec((1, 2, 1, LANES), lambda h: (h, 0, 0, 0))
    keys = pl.BlockSpec((2, SIDE, 128), lambda h: (0, 0, h))
    return pl.pallas_call(
        attend_back_kernel,
        grid=(KEY_HEADS,),
        out_shape=(
            jax.ShapeDtypeStruct((KEY_HEADS, 2, HEAD_SIZE, LANES), jnp.float32),
            jax.ShapeDtypeStruct(kv.shape, jnp.bfloat16),
        ),
        in_specs=[keys, per_head, per_head, row, row],
        out_specs=(pl.BlockSpec((1, 2, HEAD_SIZE, LANES), lambda h: (h, 0, 0, 0)), keys),
        scratch_shapes=[pltpu.VMEM((128, LANES), jnp.float32)],
        compiler_params=pltpu.CompilerParams(vmem_limit_bytes=VMEM_LIMIT),
        name="attend_back",
    )(kv, q, do, lse, delta)


def rotary_tables(positions):
    half = HEAD_SIZE // 2
    freq = ROPE_BASE ** (-(jnp.arange(half, dtype=jnp.float32) * 2.0 / HEAD_SIZE))
    angle = positions.astype(jnp.float32)[:, None] * freq[None, :]
    return (jnp.cos(angle)[:, None, :], jnp.sin(angle)[:, None, :])


def rotate(values, cosine, sine):
    count = values.shape[0]
    half = HEAD_SIZE // 2
    heads = values.reshape(count, -1, HEAD_SIZE)
    first = heads[..., :half]
    second = heads[..., half:]
    return jnp.concatenate(
        [first * cosine - second * sine, second * cosine + first * sine], -1
    ).reshape(count, -1)


def mm(form, left, right):
    return jnp.einsum(form, left, right, preferred_element_type=jnp.float32)


def by_head(rows):
    r = rows.reshape(2, HALF, KEY_HEADS, GROUPS, HEAD_SIZE)
    return jnp.transpose(r, (2, 0, 3, 1, 4)).reshape(KEY_HEADS, 2, LANES, HEAD_SIZE)


def by_token(heads):
    h = heads.reshape(KEY_HEADS, 2, HEAD_SIZE, GROUPS, HALF)
    return jnp.transpose(h, (1, 4, 0, 3, 2)).reshape(2 * HALF, QH * HEAD_SIZE)


def outer_kernel(left_ref, right_ref, out_ref):
    out_ref[0] = dot_tn(left_ref[...], right_ref[0]).astype(jnp.bfloat16)


def outer(left, right, steps):
    tokens, m = left.shape
    n = right.shape[-1]
    return pl.pallas_call(
        outer_kernel,
        grid=(2, steps),
        out_shape=jax.ShapeDtypeStruct((2, m, n), jnp.bfloat16),
        in_specs=[
            pl.BlockSpec((tokens, m // steps), lambda h, s: (0, s)),
            pl.BlockSpec((1, tokens, n), lambda h, s: (h, 0, 0)),
        ],
        out_specs=pl.BlockSpec((1, m // steps, n), lambda h, s: (h, s, 0)),
        compiler_params=pltpu.CompilerParams(vmem_limit_bytes=VMEM_LIMIT),
        name="outer",
    )(left, right)


def thirds(rows):
    high = rows.astype(jnp.bfloat16)
    rest = rows - high.astype(jnp.float32)
    middle = rest.astype(jnp.bfloat16)
    return high, middle, (rest - middle.astype(jnp.float32)).astype(jnp.bfloat16)


def ffn_kernel(
    first_ref, rest_ref, attn_ref, x_ref, dy_ref, gain_ref, spread_ref, spread_down_ref,
    layer_out_ref, middle_grad_ref, attn_grad_ref, attn_wide_ref, normed_ref, gate_low_ref, up_low_ref,
    inner_ref, middle_low_ref, gain_grad_ref,
    w_out, w_gate, w_up, w_down, gate_s, up_s, sems,
):
    bf, f32 = jnp.bfloat16, jnp.float32

    def fetch(dst, src, start, width, sem):
        c = pltpu.make_async_copy(src.at[:, :, :, pl.ds(start, width)], dst, sem)
        c.start()
        return c

    get_out = fetch(w_out, first_ref, 0, 512, sems.at[0])
    get_gate = fetch(w_gate, rest_ref, 0, 1280, sems.at[1])
    get_up = fetch(w_up, rest_ref, 1280, 1280, sems.at[2])
    get_down = [
        fetch(w_down.at[:, :, pl.ds(16 * g, 16), :], rest_ref, 2560 + 512 * g, 512, sems.at[3 + g])
        for g in range(3)
    ]
    real = lax.broadcasted_iota(jnp.int32, (128, 512), 1) < 480

    attn_wide = 0.0
    for h in range(2):
        attn_wide = attn_wide + dot_nn(attn_ref[h].astype(bf), spread_ref[h])
    attn_wide = attn_wide.astype(bf)
    attn_wide_ref[...] = attn_wide
    get_out.wait()
    middle, squares = [], 0.0
    for h in range(2):
        part = dot_nn(attn_wide, w_out[h].reshape(1024, 512))
        part = x_ref[h].astype(f32) + jnp.where(real, part, 0.0)
        squares = squares + jnp.sum(part * part, -1, keepdims=True)
        middle.append(part)
    factor = lax.rsqrt(squares / 960 + EPS)
    normed = 0.0
    for h in range(2):
        normed = normed + dot_nn((middle[h] * factor * gain_ref[h]).astype(bf), spread_ref[h])
    normed = normed.astype(bf)
    normed_ref[...] = normed
    get_gate.wait()
    get_up.wait()
    for h in range(2):
        gate = dot_nn(normed, w_gate[h].reshape(1024, 1280))
        up = dot_nn(normed, w_up[h].reshape(1024, 1280))
        gate_s[h], up_s[h] = gate, up
        inner = (gate * jax.nn.sigmoid(gate) * up).astype(bf)
        for b in range(2):
            inner_ref[:, pl.ds(768 * (2 * h + b), 768)] = dot_nn(
                inner[:, 640 * b : 640 * b + 640], spread_down_ref[...]
            ).astype(bf)
    for c in get_down:
        c.wait()
    for h in range(2):
        low = dot_nn(inner_ref[...], w_down[h].reshape(3072, 512))
        layer_out_ref[h] = (middle[h] + low).astype(bf)
    normed_grad = 0.0
    for h in range(2):
        for b in range(2):
            blocks = pl.ds(16 * (2 * h + b), 16)
            wide_grad = 0.0
            for d in range(2):
                wide_grad = wide_grad + dot_nt(dy_ref[d], w_down[d, blocks].reshape(768, 512))
            inner_grad = 0.0
            for t in thirds(wide_grad):
                inner_grad = inner_grad + dot_nt(t, spread_down_ref[...])
            cols = pl.ds(640 * b, 640)
            gate, up = gate_s[h, :, cols], up_s[h, :, cols]
            sigma = jax.nn.sigmoid(gate)
            gate_low_ref[h, :, cols] = (inner_grad * up * sigma * (1.0 + gate * (1.0 - sigma))).astype(bf)
            up_low_ref[h, :, cols] = (inner_grad * (gate * sigma)).astype(bf)
        normed_grad = normed_grad + dot_nt(gate_low_ref[h], w_gate[h].reshape(1024, 1280))
        normed_grad = normed_grad + dot_nt(up_low_ref[h], w_up[h].reshape(1024, 1280))
    split = thirds(normed_grad)
    grads, mean = [], 0.0
    for h in range(2):
        g = 0.0
        for t in split:
            g = g + dot_nt(t, spread_ref[h])
        gain_grad_ref[h] = jnp.sum(g * middle[h] * factor, 0, keepdims=True)
        g = g * gain_ref[h]
        mean = mean + jnp.sum(g * middle[h], -1, keepdims=True)
        grads.append(g)
    wide_grad = 0.0
    for h in range(2):
        total = dy_ref[h].astype(f32) + factor * grads[h] - middle[h] * (factor * factor * factor * (mean / 960))
        middle_grad_ref[h] = total
        middle_low_ref[h] = total.astype(bf)
        wide_grad = wide_grad + dot_nt(total.astype(bf), w_out[h].reshape(1024, 512))
    wide_grad = wide_grad.astype(bf)
    for h in range(2):
        attn_grad_ref[h] = dot_nt(wide_grad, spread_ref[h]).astype(bf)


def ffn(first, rest, attn, x, dy, gain, spread, spread_down):
    bf, f32 = jnp.bfloat16, jnp.float32
    vmem = pl.BlockSpec(memory_space=pltpu.VMEM)
    shapes = [
        ((2, 128, 512), bf), ((2, 128, 512), f32), ((2, 128, 512), bf), ((128, 1024), bf), ((128, 1024), bf),
        ((2, 128, 1280), bf), ((2, 128, 1280), bf), ((128, 3072), bf), ((2, 128, 512), bf), ((2, 1, 512), f32),
    ]
    return pl.pallas_call(
        ffn_kernel,
        out_shape=tuple(jax.ShapeDtypeStruct(s, d) for s, d in shapes),
        in_specs=[pl.BlockSpec(memory_space=pl.ANY)] * 2 + [vmem] * 6,
        out_specs=(vmem,) * len(shapes),
        scratch_shapes=[
            pltpu.VMEM((2, 64, 16, 512), bf),
            pltpu.VMEM((2, 64, 16, 1280), bf),
            pltpu.VMEM((2, 64, 16, 1280), bf),
            pltpu.VMEM((2, 64, 48, 512), bf),
            pltpu.VMEM((2, 128, 1280), f32),
            pltpu.VMEM((2, 128, 1280), f32),
            pltpu.SemaphoreType.DMA((6,)),
        ],
        compiler_params=pltpu.CompilerParams(vmem_limit_bytes=VMEM_LIMIT),
        name="ffn",
    )(first, rest, attn, x, dy, gain, spread, spread_down)


def halves(rows):
    both = jnp.stack([rows[:, :480], rows[:, 480:]])
    return jnp.pad(both, ((0, 0), (0, 0), (0, 32)))


def joined(both):
    return jnp.concatenate([both[0, :, :480], both[1, :, :480]], 1)


def local(
    layer_in,
    attn_gain,
    query_weight,
    key_weight,
    value_weight,
    output_weight,
    ffn_gain,
    gate_weight,
    up_weight,
    down_weight,
    out_cotangent,
):
    bf, f32 = jnp.bfloat16, jnp.float32
    me = my_block()

    gains = jnp.pad(jnp.concatenate([attn_gain, ffn_gain])[None], ((0, 0), (0, 1250)))
    oqkv = jnp.concatenate([output_weight, query_weight, key_weight, value_weight], 1)
    first, x_low, dy = gather(
        jnp.concatenate([oqkv, gains], 0), W_DIMS, FIRST_PARTS, "gather_first", 1, (layer_in, out_cotangent)
    )
    first = first.reshape(2, 64, 16, 1280)
    w_qkv = first.reshape(2, 1024, 1280)[:, :, 480:]
    gain_one = jnp.pad(first[0, :, 15, :15], ((0, 0), (0, 1))).reshape(1024).astype(f32)
    gain_two = first[0, :, 15, 15:30].reshape(1, 960).astype(f32)
    down = jnp.pad(down_weight, ((0, 8), (0, 32))).reshape(3, 16, 512)
    wide = jnp.pad(jnp.concatenate([gate_weight, up_weight], 1), ((0, 1), (0, 0)))
    rest = jnp.concatenate([wide, down[0], down[1], down[2]], 1)

    i = lax.broadcasted_iota(jnp.int32, (2, 512, 1024), 1)
    d = i + 480 * lax.broadcasted_iota(jnp.int32, (2, 512, 1024), 0)
    j = lax.broadcasted_iota(jnp.int32, (2, 512, 1024), 2)
    spread = jnp.logical_and(i < 480, j == (d // 15) * 16 + d % 15).astype(bf)
    i = lax.broadcasted_iota(jnp.int32, (640, 768), 0)
    j = lax.broadcasted_iota(jnp.int32, (640, 768), 1)
    spread_down = (j == (i // 40) * 48 + i % 40).astype(bf)

    t = jnp.arange(HALF, dtype=jnp.int32)
    positions = jnp.concatenate([me * 128 + t, (BLOCKS - 1 - me) * 128 + HALF + t])
    cosine, sine = rotary_tables(positions)

    x_halves, dy_halves = halves(x_low), halves(dy)
    hidden = mm("htd,hde->te", x_halves, spread)
    factor_one = lax.rsqrt(jnp.sum(hidden * hidden, -1, keepdims=True) / 960 + EPS)
    normed = (hidden * factor_one * gain_one).astype(bf)
    qkv = mm("te,hec->thc", normed, w_qkv)
    query = qkv[:, :, :480].reshape(128, 960)
    key = qkv[:, :, 480:640].reshape(128, 320)
    value = qkv[:, :, 640:800].reshape(128, 320)
    query_rot = rotate(query, cosine, sine).astype(bf)
    key_rot = rotate(key, cosine, sine).astype(bf)
    kv_piece = jnp.concatenate(
        [key_rot.reshape(2, HALF, KEY_HEADS, 64), value.astype(bf).reshape(2, HALF, KEY_HEADS, 64)], -1
    ).reshape(2, HALF, 640)
    (kv,) = gather(kv_piece, T_DIMS, T_PARTS, "gather_keys", 2)
    kv = kv.reshape(2, SIDE, 640)
    q_heads = jnp.pad(by_head(query_rot * jnp.asarray(0.125, bf)), ((0, 0), (0, 0), (0, 0), (0, 64)))
    attn_heads, lse, rest = attend(kv, q_heads, rest)
    rest = rest.reshape(2, 64, 16, 4096)
    attn = by_token(attn_heads)
    (layer_out, middle_grad, attn_grad, attn_wide, normed_two, gate_low, up_low, inner, middle_low, gain_two_term) = ffn(
        first, rest, halves(attn), x_halves, dy_halves, halves(gain_two), spread, spread_down
    )
    layer_out, middle_grad, attn_grad = joined(layer_out), joined(middle_grad), joined(attn_grad)
    delta = jnp.sum((attn_grad.astype(f32) * attn).reshape(2, HALF, KEY_HEADS, GROUPS, HEAD_SIZE), -1)
    delta = jnp.transpose(delta, (2, 0, 3, 1)).reshape(KEY_HEADS, 2, 1, LANES)
    do_heads = jnp.pad(by_head(attn_grad), ((0, 0), (0, 0), (0, 0), (64, 0)))
    dq_heads, dkv = attend_back(kv, q_heads, do_heads, lse, delta)
    dkv = dkv.reshape(2, 2, 4, 4, 2, 2, HALF, 640)
    parts = tuple(((0, c, 0, ALL),) for c in T_PARTS)
    key_sums, layer_out = scatter([dkv], T_DIMS, parts, HALF, "scatter_keys", 3, VMEM_LIMIT, (layer_out,))
    key_sums = key_sums.reshape(128, KEY_HEADS, 128)
    query_low = rotate(by_token(dq_heads) * 0.125, cosine, -sine).astype(bf)
    key_low = rotate(key_sums[..., :64].reshape(128, 320), cosine, -sine).astype(bf)
    value_low = key_sums[..., 64:].reshape(128, 320).astype(bf)
    qkv_low = jnp.concatenate(
        [query_low.reshape(128, 2, 480), key_low.reshape(128, 2, 160), value_low.reshape(128, 2, 160)], -1
    )
    normed_grad = mm("thc,hec->te", qkv_low, w_qkv)
    weighted = gain_one * normed_grad
    input_back = factor_one * weighted - hidden * factor_one**3 * (
        jnp.sum(weighted * hidden, -1, keepdims=True) / 960
    )
    gain_one_term = jnp.sum(normed_grad * hidden * factor_one, 0)
    input_back = sum(mm("te,hde->htd", part, spread) for part in thirds(input_back))
    input_grad = middle_grad + joined(input_back)

    gains = jnp.concatenate([gain_one_term.reshape(64, 16)[:, :15], joined(gain_two_term).reshape(64, 15)], 1)
    gains = jnp.pad(gains.astype(bf), ((0, 0), (0, 1280 - 30)))
    right = jnp.concatenate(
        [
            jnp.pad(jnp.transpose(qkv_low, (1, 0, 2)), ((0, 0), (0, 0), (480, 0))),
            jnp.pad(middle_low[:, :, :480], ((0, 0), (0, 0), (0, 800))),
            jnp.stack([gains, gains]),
        ],
        1,
    )
    slot = lax.broadcasted_iota(jnp.int32, (64, 1024), 0) * 16 + 15
    slot = (slot == lax.broadcasted_iota(jnp.int32, (64, 1024), 1)).astype(bf)
    left = jnp.concatenate([normed, attn_wide, slot], 0)
    terms = [outer(normed_two, gate_low, 1), outer(normed_two, up_low, 1), outer(left, right, 1)]
    terms = [a.reshape(2, 2, 4, 4, 2, 16, 1280) for a in terms]
    terms.append(outer(inner, dy_halves, 1).reshape(2, 2, 4, 4, 2, 48, 512))
    parts = tuple(((k, (0, 1280), 0, ALL), (3, (0, 512), 1280, pl.ds(16 * k, 16))) for k in range(3))
    sums, input_grad = scatter(terms, W_DIMS, parts, 16, "scatter_weights", 4, VMEM_LIMIT, (input_grad,))
    down_sum = jnp.concatenate([sums[:, 1280:1792], sums[:, 3072:3584], sums[:, 4864:5376]], 0)
    return (
        layer_out,
        input_grad,
        sums[15, 3584:3599],
        sums[:15, 4064:4544],
        sums[:15, 4544:4704],
        sums[:15, 4704:4864],
        sums[:15, 3584:4064],
        sums[15, 3599:3614],
        sums[:15, :1280],
        sums[:15, 1792:3072],
        down_sum[:40, :480],
    )


def solution(mesh):
    matrix, tokens = P("ctx", "fsdp"), P(("ctx", "fsdp"), None)
    return jax.shard_map(
        local,
        mesh=mesh,
        in_specs=(tokens, P("ctx"), matrix, matrix, matrix, matrix, P("ctx"), matrix, matrix, matrix, tokens),
        out_specs=(tokens, tokens, P("ctx"), matrix, matrix, matrix, matrix, P("ctx"), matrix, matrix, matrix),
        check_vma=False,
    )
```
